32 devices in a mesh: ctx: 8 (over z, x), ch: 4 (over y, core).
Axes of the slice: x: 2, y: 2, z: 4, core: 2. Of those that a mesh axis runs over, the one named last changes fastest.
Arguments:
- signal: bfloat16 [2048, 4096], P('ctx', 'ch'), may hold values from -6 to 6
- upstream: bfloat16 [2048, 8192], P('ctx', 'ch'), may hold values from -6 to 6
- out_weight: bfloat16 [4096, 8192], P(None, 'ch'), may hold values from -0.0625 to 0.0625
- residues: float32 [4096, 16], P('ch'), may hold values from -6 to 6
- decays: float32 [4096, 16], P('ch'), may hold values from 0.5 to 300
- skip_gain: float32 [4096], P('ch'), may hold values from 0.2 to 1
Outputs:
- grad_signal: bfloat16 [2048, 4096], P('ctx', 'ch')
- grad_residues: float32 [4096, 16], P('ch')
- grad_decays: float32 [4096, 16], P('ch')
- grad_skip: float32 [4096], P('ch')
The draws below stay inside these ranges and needn't reach their ends.
All inputs are finite; a program needn't handle non-finite values.
Results may differ from the reference program's by a relative error of at most 0.019.
Values may be sent and summed in bfloat16 or wider, within the bound.
No kernel may reach another device: no remote copies, remote signals or barrier semaphores. Data moves between devices by JAX's collectives and lax.ppermute only.
A program may use at most 128 MiB of HBM per device.

```python
import math
import jax
import jax.numpy as jnp
from jax import lax

D = 4096
DOUT = 8192
ORDER = 16
SEQ = 2048
N_CH = 4


def levels(stream_key, shape, split, low, top_value):
    gain = 1.0
    for dim, blocks in split:
        heights = jax.random.uniform(jax.random.fold_in(jax.random.fold_in(stream_key, 6), dim), (blocks,), jnp.float32, low / len(split), top_value / len(split))
        gain = gain * jnp.repeat(jnp.exp(heights), shape[dim] // blocks).reshape((-1,) + (1,) * (len(shape) - 1 - dim))
    return gain


def normal_values(rng, shape, deviation, reach, cuts=(), held_as=jnp.bfloat16):
    gain = levels(rng, shape, cuts, -0.22, 0.18) if cuts else 1.0
    drawn = jax.random.normal(rng, shape, jnp.float32) * deviation * gain
    return jnp.minimum(jnp.maximum(drawn, -reach), reach).astype(held_as)


def setup_inputs(seed: int = 0) -> dict:
    streams_of = jax.random.split(jax.random.key(seed), 7)
    return {
        "signal": normal_values(streams_of[0], (SEQ, D), 1.0, 6.0, ((0, 8), (1, 4))),
        "upstream": normal_values(streams_of[1], (SEQ, DOUT), 1.0, 6.0, ((0, 8), (1, 4))),
        "out_weight": normal_values(streams_of[2], (D, DOUT), DOUT ** -0.5, 0.0625, ((1, 4),)),
        "residues": normal_values(streams_of[3], (D, ORDER), 1.0, 6.0, ((0, 4),), jnp.float32),
        "decays": jnp.clip(jnp.exp(math.log(300.0) - 6.3969297 * jax.random.uniform(streams_of[4], (D, ORDER), jnp.float32) ** levels(streams_of[4], (D, ORDER), ((0, 4),), -0.2, 0.2)), 0.5, 300.0),
        "skip_gain": jnp.clip(0.2 + 0.8 * jax.random.uniform(streams_of[5], (D,), jnp.float32) ** levels(streams_of[5], (D,), ((0, 4),), -0.2, 0.2), 0.2, 1.0),
    }


def reference(signal, upstream, out_weight, residues, decays, skip_gain):
    block = DOUT // N_CH
    total = jnp.zeros((SEQ, D), jnp.float32)
    for index in range(N_CH):
        part = jnp.dot(upstream[:, index * block:(index + 1) * block], out_weight[:, index * block:(index + 1) * block].T, preferred_element_type=jnp.float32)
        part = lax.optimization_barrier(part.astype(jnp.bfloat16))
        total = total + part.astype(jnp.float32)
    grad_conv = total.astype(jnp.bfloat16).astype(jnp.float32)
    sig = signal.astype(jnp.float32)
    padded = 2 * SEQ
    frac = jnp.arange(SEQ, dtype=jnp.float32) / SEQ
    filt = jnp.zeros((SEQ, D), jnp.float32)
    for mode in range(ORDER):
        filt = filt + residues[:, mode][None, :] * jnp.exp(-decays[:, mode][None, :] * frac[:, None])
    filt = filt / jnp.sqrt(jnp.float32(SEQ))
    spec_conv = jnp.fft.rfft(grad_conv, n=padded, axis=0)
    spec_sig = jnp.fft.rfft(sig, n=padded, axis=0)
    spec_filt = jnp.fft.rfft(filt, n=padded, axis=0)
    conv_back = jnp.fft.irfft(jnp.conj(spec_filt) * spec_conv, n=padded, axis=0)[:SEQ]
    grad_signal = (conv_back + skip_gain[None, :] * grad_conv).astype(jnp.bfloat16)
    grad_filt = jnp.fft.irfft(jnp.conj(spec_sig) * spec_conv, n=padded, axis=0)[:SEQ]
    res_cols = []
    dec_cols = []
    for mode in range(ORDER):
        power = jnp.exp(-decays[:, mode][None, :] * frac[:, None])
        res_cols.append(lax.optimization_barrier(jnp.sum(grad_filt * power, axis=0)) / SEQ)
        dec_cols.append(-residues[:, mode] * lax.optimization_barrier(jnp.sum(grad_filt * power * frac[:, None], axis=0)) / SEQ)
    grad_residues = jnp.stack(res_cols, axis=1).astype(jnp.float32)
    grad_decays = jnp.stack(dec_cols, axis=1).astype(jnp.float32)
    grad_skip = (lax.optimization_barrier(jnp.sum(grad_conv * sig, axis=0)) / jnp.sqrt(jnp.float32(SEQ))).astype(jnp.float32)
    return (grad_signal, grad_residues, grad_decays, grad_skip)
```

```python
import functools
import math

import jax
import jax.numpy as jnp
from jax import lax
from jax.experimental import pallas as pl
from jax.experimental.pallas import tpu as pltpu
from jax.sharding import PartitionSpec as P

F32 = jnp.float32
BF16 = jnp.bfloat16
SUB = 8
LANES = 128
VMEM_LIMIT = 48 * 1024 * 1024


def interleave(tokens, transpose=False):
    steps = tokens // SUB
    row = lax.broadcasted_iota(jnp.int32, (tokens, tokens), 1 if transpose else 0)
    col = lax.broadcasted_iota(jnp.int32, (tokens, tokens), 0 if transpose else 1)
    return jnp.where(col == (row % SUB) * steps + row // SUB, 1.0, 0.0).astype(BF16)


def params():
    return pltpu.CompilerParams(vmem_limit_bytes=VMEM_LIMIT)


def whole(ref):
    return pl.BlockSpec(memory_space=pltpu.VMEM)


def order_kernel(up_ref, o_ref):
    o_ref[...] = jnp.dot(
        interleave(up_ref.shape[0]), up_ref[...], preferred_element_type=F32
    ).astype(BF16)


def reorder(x):
    return pl.pallas_call(
        order_kernel,
        out_shape=jax.ShapeDtypeStruct(x.shape, BF16),
        in_specs=[whole(x)],
        out_specs=whole(x),
        compiler_params=params(),
        name="reorder",
    )(x)


def project_kernel(added, blk_ref, up_ref, w_ref, *refs):
    o_ref = refs[-1]
    part = lax.dot_general(
        up_ref[...], w_ref[...], (((1,), (1,)), ((), ())), preferred_element_type=F32
    )
    if added:
        part = part + refs[0][...].astype(F32)
    o_ref[...] = part.astype(o_ref.dtype)


def project(up, weight, block, width, extra, dtype):
    tokens, feats = up.shape
    rows = min(256, width)
    per = width // rows
    in_specs = [
        pl.BlockSpec((tokens, feats), lambda s, b: (0, 0)),
        pl.BlockSpec((rows, feats), lambda s, b: (b[0] * per + s, 0)),
    ]
    args = [up, weight]
    if extra is not None:
        in_specs.append(pl.BlockSpec((tokens, rows), lambda s, b: (0, s)))
        args.append(extra)
    return pl.pallas_call(
        functools.partial(project_kernel, extra is not None),
        out_shape=jax.ShapeDtypeStruct((tokens, width), dtype),
        grid_spec=pltpu.PrefetchScalarGridSpec(
            num_scalar_prefetch=1,
            grid=(per,),
            in_specs=in_specs,
            out_specs=pl.BlockSpec((tokens, rows), lambda s, b: (0, s)),
        ),
        compiler_params=params(),
        cost_estimate=pl.CostEstimate(
            flops=2 * tokens * feats * width,
            bytes_accessed=2 * feats * (width + tokens),
            transcendentals=0,
        ),
        name="project",
    )(jnp.reshape(block, (1,)).astype(jnp.int32), *args)


def bcast(row):
    return jnp.broadcast_to(row, (SUB, row.shape[-1]))


def signal_kernel(length, sig_ref, dec_ref, sigp_ref, y_ref, y1_ref, end_ref, sp, ebuf, e1buf):
    tokens, width = sig_ref.shape
    modes = dec_ref.shape[0]
    steps = tokens // SUB
    ordered = jnp.dot(interleave(tokens), sig_ref[...], preferred_element_type=F32)
    sigp_ref[...] = ordered.astype(BF16)
    sp[...] = ordered
    half = modes // 2

    @pl.loop(0, width // LANES)
    def _(block):
        lanes = pl.ds(pl.multiple_of(block * LANES, LANES), LANES)
        rate = dec_ref[:, lanes] * (1.0 / length)
        pole = jnp.exp(-rate)
        pole_sub = jnp.exp(-rate * steps)
        for first in (0, half):
            poles = [bcast(pole[n : n + 1]) for n in range(first, first + half)]

            def step(i, state):
                ends, firsts = state
                value = sp[pl.ds(pl.multiple_of(i * SUB, SUB), SUB), lanes]
                ends = [p * (e + value) for p, e in zip(poles, ends)]
                firsts = [p * f + e for p, f, e in zip(poles, firsts, ends)]
                return ends, firsts

            zeros = [jnp.zeros((SUB, LANES), F32)] * half
            ends, firsts = lax.fori_loop(0, steps, step, (zeros, zeros), unroll=4)
            for n in range(half):
                ebuf[pl.ds((first + n) * SUB, SUB), :] = ends[n]
                e1buf[pl.ds((first + n) * SUB, SUB), :] = firsts[n]
        carry = jnp.zeros((modes, LANES), F32)
        carry1 = jnp.zeros((modes, LANES), F32)
        for j in range(SUB):
            y_ref[j, :, lanes] = carry
            y1_ref[j, :, lanes] = carry1
            carry1 = pole_sub * (carry1 + steps * carry) + e1buf[pl.ds(j, modes, stride=SUB), :]
            carry = pole_sub * carry + ebuf[pl.ds(j, modes, stride=SUB), :]
        end_ref[0:modes, lanes] = carry
        end_ref[modes : 2 * modes, lanes] = carry1


def signal_states(signal, decays, length):
    tokens, width = signal.shape
    modes = decays.shape[0]
    return pl.pallas_call(
        functools.partial(signal_kernel, length),
        out_shape=(
            jax.ShapeDtypeStruct((tokens, width), BF16),
            jax.ShapeDtypeStruct((SUB, modes, width), F32),
            jax.ShapeDtypeStruct((SUB, modes, width), F32),
            jax.ShapeDtypeStruct((2 * modes, width), F32),
        ),
        in_specs=[whole(None)] * 2,
        out_specs=(whole(None),) * 4,
        scratch_shapes=[
            pltpu.VMEM((tokens, width), F32),
            pltpu.VMEM((modes * SUB, LANES), F32),
            pltpu.VMEM((modes * SUB, LANES), F32),
        ],
        compiler_params=params(),
        cost_estimate=pl.CostEstimate(
            flops=4 * modes * tokens * width, bytes_accessed=8 * tokens * width, transcendentals=0
        ),
        name="signal_states",
    )(signal, decays)


def gradient_kernel(
    length, own_ref, got_ref, sigp_ref, dec_ref, res_ref, y_ref, y1_ref, ydev_ref,
    loc_ref, grad_ref, carry_ref, pay_ref, gs, ss, zero, sbuf, s1buf, abuf, a1buf,
):
    tokens, width = sigp_ref.shape
    modes = dec_ref.shape[0]
    steps = tokens // SUB
    half = modes // 2
    zero[...] = jnp.zeros_like(zero)

    @pl.loop(0, width // LANES)
    def _(block):
        lanes = pl.ds(pl.multiple_of(block * LANES, LANES), LANES)
        total = own_ref[:, lanes]
        for q in range(got_ref.shape[0]):
            total = total + got_ref[q, :, lanes].astype(F32)
        total = total.astype(BF16)
        grad_ref[:, lanes] = total
        gs[...] = total.astype(F32)
        ss[...] = sigp_ref[:, lanes].astype(F32)
        pay_ref[3 * modes : 3 * modes + SUB, lanes] = bcast(
            jnp.sum(gs[...] * ss[...], axis=0, keepdims=True)
        )
        rate = dec_ref[:, lanes] * (1.0 / length)
        pole = jnp.exp(-rate)
        pole_sub = jnp.exp(-rate * steps)
        weight = res_ref[:, lanes]
        for first in (0, half):
            poles = [bcast(pole[n : n + 1]) for n in range(first, first + half)]
            weights = [bcast(weight[n : n + 1]) for n in range(first, first + half)]

            def step(t, state):
                hs, ks, res, dec = state
                rows = pl.ds(pl.multiple_of((steps - 1 - t) * SUB, SUB), SUB)
                value = gs[rows, :]
                seen = ss[rows, :]
                ks = [p * (k + h) for p, k, h in zip(poles, ks, hs)]
                hs = [p * h + value for p, h in zip(poles, hs)]
                res = [a + seen * h for a, h in zip(res, hs)]
                dec = [a + seen * k for a, k in zip(dec, ks)]
                terms = [r * h for r, h in zip(weights, hs)]
                while len(terms) > 1:
                    terms = [a + b for a, b in zip(terms[::2], terms[1::2])]
                if first == 0:
                    loc_ref[rows, lanes] = terms[0]
                else:
                    loc_ref[rows, lanes] = loc_ref[rows, lanes] + terms[0]
                return hs, ks, res, dec

            zeros = [zero[...]] * half
            hs, ks, res, dec = lax.fori_loop(0, steps, step, (zeros,) * 4, unroll=2)
            for n in range(half):
                rows = pl.ds((first + n) * SUB, SUB)
                sbuf[rows, :] = hs[n]
                s1buf[rows, :] = ks[n]
                abuf[rows, :] = res[n]
                a1buf[rows, :] = dec[n]
        carry = jnp.zeros((modes, LANES), F32)
        carry1 = jnp.zeros((modes, LANES), F32)
        res_sum = jnp.zeros((modes, LANES), F32)
        dec_sum = jnp.zeros((modes, LANES), F32)
        for j in reversed(range(SUB)):
            pick = pl.ds(j, modes, stride=SUB)
            start = sbuf[pick, :]
            start1 = s1buf[pick, :]
            before = y_ref[j, :, lanes]
            before1 = y1_ref[j, :, lanes]
            res_sum = res_sum + abuf[pick, :] + start * before
            dec_sum = dec_sum + a1buf[pick, :] + start1 * before + start * before1
            carry_ref[j, :, lanes] = carry
            carry1 = start1 + pole_sub * (carry1 + steps * carry)
            carry = start + pole_sub * carry
        before = ydev_ref[0:modes, lanes]
        before1 = ydev_ref[modes : 2 * modes, lanes]
        pay_ref[0:modes, lanes] = carry
        pay_ref[modes : 2 * modes, lanes] = res_sum + carry * before
        pay_ref[2 * modes : 3 * modes, lanes] = dec_sum + carry1 * before + carry * before1


def gradient_states(own, got, sigp, decays, residues, y, y1, ydev, length):
    tokens, width = sigp.shape
    modes = decays.shape[0]
    return pl.pallas_call(
        functools.partial(gradient_kernel, length),
        out_shape=(
            jax.ShapeDtypeStruct((tokens, width), F32),
            jax.ShapeDtypeStruct((tokens, width), BF16),
            jax.ShapeDtypeStruct((SUB, modes, width), F32),
            jax.ShapeDtypeStruct((3 * modes + SUB, width), F32),
        ),
        in_specs=[whole(None)] * 8,
        out_specs=(whole(None),) * 4,
        scratch_shapes=[
            pltpu.VMEM((tokens, LANES), F32),
            pltpu.VMEM((tokens, LANES), F32),
            pltpu.VMEM((SUB, LANES), F32),
            pltpu.VMEM((modes * SUB, LANES), F32),
            pltpu.VMEM((modes * SUB, LANES), F32),
            pltpu.VMEM((modes * SUB, LANES), F32),
            pltpu.VMEM((modes * SUB, LANES), F32),
        ],
        compiler_params=params(),
        cost_estimate=pl.CostEstimate(
            flops=10 * modes * tokens * width, bytes_accessed=16 * tokens * width, transcendentals=0
        ),
        name="gradient_states",
    )(own, got, sigp, decays, residues, y, y1, ydev)


def finish_kernel(
    length, loc_ref, grad_ref, carry_ref, later_ref, dec_ref, res_ref, gain_ref, sums_ref,
    o_ref, ores_ref, odec_ref, oskip_ref, vals, cbuf,
):
    tokens, width = loc_ref.shape
    modes = dec_ref.shape[0]
    steps = tokens // SUB
    scale = 1.0 / math.sqrt(length)

    @pl.loop(0, width // LANES)
    def _(block):
        lanes = pl.ds(pl.multiple_of(block * LANES, LANES), LANES)
        rate = dec_ref[:, lanes] * (1.0 / length)
        pole = jnp.exp(-rate)
        pole_sub = jnp.exp(-rate * steps)
        weight = res_ref[:, lanes]
        later = later_ref[:, lanes]
        for j in reversed(range(SUB)):
            cbuf[pl.ds(j, modes, stride=SUB), :] = weight * (carry_ref[j, :, lanes] + later)
            later = later * pole_sub
        poles = [bcast(pole[n : n + 1]) for n in range(modes)]
        start = [cbuf[pl.ds(n * SUB, SUB), :] for n in range(modes)]
        gain = bcast(gain_ref[:, lanes])

        def step(t, state):
            first = steps - 2 - 2 * t
            both = pl.ds(pl.multiple_of(first * SUB, 2 * SUB), 2 * SUB)
            outs = []
            for _ in range(2):
                state = [p * e for p, e in zip(poles, state)]
                terms = state
                while len(terms) > 1:
                    terms = [a + b for a, b in zip(terms[::2], terms[1::2])]
                outs.append(terms[0])
            more = jnp.concatenate(outs[::-1], axis=0)
            grad = grad_ref[both, lanes].astype(F32)
            skip = jnp.concatenate([gain, gain], axis=0) * grad
            vals[both, lanes] = ((loc_ref[both, lanes] + more) * scale + skip).astype(BF16)
            return state

        lax.fori_loop(0, steps // 2, step, start, unroll=2)

    o_ref[...] = jnp.dot(
        interleave(tokens, transpose=True), vals[...], preferred_element_type=F32
    ).astype(BF16)
    ores_ref[...] = (sums_ref[modes : 2 * modes, :] * (1.0 / length)).T
    odec_ref[...] = (
        sums_ref[2 * modes : 3 * modes, :] * (-1.0 / (length * length)) * res_ref[...]
    ).T
    oskip_ref[...] = sums_ref[3 * modes : 3 * modes + 1, :] * scale


def finish(loc, grad, carry, later, decays, residues, gain, sums, length):
    tokens, width = loc.shape
    modes = decays.shape[0]
    return pl.pallas_call(
        functools.partial(finish_kernel, length),
        out_shape=(
            jax.ShapeDtypeStruct((tokens, width), BF16),
            jax.ShapeDtypeStruct((width, modes), F32),
            jax.ShapeDtypeStruct((width, modes), F32),
            jax.ShapeDtypeStruct((1, width), F32),
        ),
        in_specs=[whole(None)] * 8,
        out_specs=(whole(None),) * 4,
        scratch_shapes=[
            pltpu.VMEM((tokens, width), BF16),
            pltpu.VMEM((modes * SUB, LANES), F32),
        ],
        compiler_params=params(),
        cost_estimate=pl.CostEstimate(
            flops=2 * modes * tokens * width, bytes_accessed=10 * tokens * width, transcendentals=0
        ),
        name="finish",
    )(loc, grad, carry, later, decays, residues, gain, sums)


def send(x, axis, size, hop):
    return lax.ppermute(x, axis, [(i, i ^ hop) for i in range(size)])


def prefix_over_ctx(ends, rate, length, tokens, groups, modes):
    me = lax.axis_index("ctx")
    state, first = ends[:modes], ends[modes:]
    before = jnp.zeros_like(state)
    before1 = jnp.zeros_like(state)
    hop = 1
    while hop < groups:
        there = send(jnp.concatenate([state, first]).astype(BF16), "ctx", groups, hop).astype(F32)
        other, other1 = there[:modes], there[modes:]
        inside = (me & (hop - 1)).astype(F32)
        upper = (me & hop) != 0
        reach = jnp.exp(-rate * (inside * tokens))
        before = before + jnp.where(upper, reach * other, 0.0)
        before1 = before1 + jnp.where(upper, reach * (other1 + (inside * tokens) * other), 0.0)
        span = jnp.exp(-rate * (hop * tokens))
        late = jnp.where(upper, state, other)
        late1 = jnp.where(upper, first, other1)
        early = jnp.where(upper, other, state)
        early1 = jnp.where(upper, other1, first)
        first = late1 + span * (early1 + (hop * tokens) * early)
        state = late + span * early
        hop *= 2
    return jnp.concatenate([before, before1])


def suffix_over_ctx(pay, rate, tokens, groups, modes):
    me = lax.axis_index("ctx")
    state, sums = pay[:modes], pay[modes:]
    later = jnp.zeros_like(state)
    hop = 1
    while hop < groups:
        there = send(jnp.concatenate([state, sums]).astype(BF16), "ctx", groups, hop).astype(F32)
        other, other_sums = there[:modes], there[modes:]
        inside = (me & (hop - 1)).astype(F32)
        lower = (me & hop) == 0
        reach = jnp.exp(-rate * ((hop - 1 - inside) * tokens))
        later = later + jnp.where(lower, reach * other, 0.0)
        span = jnp.exp(-rate * (hop * tokens))
        early = jnp.where(lower, state, other)
        late = jnp.where(lower, other, state)
        state = early + span * late
        sums = sums + other_sums
        hop *= 2
    return later, sums


def body(signal, upstream, out_weight, residues, decays, skip_gain):
    tokens, width = signal.shape
    groups = lax.axis_size("ctx")
    blocks = lax.axis_size("ch")
    length = tokens * groups
    modes = residues.shape[1]
    me = lax.axis_index("ch")
    dec = decays.T
    res = residues.T
    rate = dec * (1.0 / length)

    up = reorder(upstream)
    arrived = []
    for hop in range(2, blocks, 2):
        lent = project(up, out_weight, me ^ hop ^ 1, width, None, BF16)
        lent = send(lent, "ch", blocks, 1)
        pair = project(up, out_weight, me ^ hop, width, lent, BF16)
        arrived.append(send(pair, "ch", blocks, hop))
    lent = project(up, out_weight, me ^ 1, width, None, BF16)
    lent = send(lent, "ch", blocks, 1)
    own = project(up, out_weight, me, width, lent, F32)

    sigp, y, y1, ends = signal_states(signal, dec, length)
    ydev = prefix_over_ctx(ends, rate, length, tokens, groups, modes)
    loc, grad, carry, pay = gradient_states(
        own, jnp.stack(arrived), sigp, dec, res, y, y1, ydev, length
    )
    later, sums = suffix_over_ctx(pay, rate, tokens, groups, modes)
    out, ores, odec, oskip = finish(
        loc, grad, carry, later, dec, res, skip_gain[None, :],
        jnp.concatenate([jnp.zeros_like(later), sums]), length,
    )
    return (out, ores, odec, oskip[0])


def solution(mesh):
    placed = (P("ctx", "ch"), P("ctx", "ch"), P(None, "ch"), P("ch", None), P("ch", None), P("ch"))
    return jax.shard_map(
        body,
        mesh=mesh,
        in_specs=placed,
        out_specs=(P("ctx", "ch"), P("ch", None), P("ch", None), P("ch")),
        check_vma=False,
    )
```

```python
import functools
import math

import jax
import jax.numpy as jnp
from jax import lax
from jax.experimental import pallas as pl
from jax.experimental.pallas import tpu as pltpu
from jax.sharding import PartitionSpec as P

F32 = jnp.float32
BF16 = jnp.bfloat16
SUB = 16
HALF = 8
LANES = 128
VMEM_LIMIT = 12 * 1024 * 1024
PROJECT_LIMIT = 50 * 1024 * 1024
VM = pl.BlockSpec(memory_space=pltpu.VMEM)
SM = pl.BlockSpec(memory_space=pltpu.SMEM)


def interleave(tokens, transpose=False):
    steps = tokens // SUB
    row = lax.broadcasted_iota(jnp.int32, (tokens, tokens), 1 if transpose else 0)
    col = lax.broadcasted_iota(jnp.int32, (tokens, tokens), 0 if transpose else 1)
    return jnp.where(col == (row % SUB) * steps + row // SUB, 1.0, 0.0).astype(BF16)


def group_sums(groups, size):
    col = lax.broadcasted_iota(jnp.int32, (groups, groups * size), 1)
    row = lax.broadcasted_iota(jnp.int32, (groups, groups * size), 0)
    return jnp.where(col // size == row, 1.0, 0.0).astype(F32)


def params(limit=VMEM_LIMIT):
    return pltpu.CompilerParams(vmem_limit_bytes=limit)


SMALL = pl.CostEstimate(flops=1, bytes_accessed=1, transcendentals=0)


def spread(row):
    return jnp.broadcast_to(row, (HALF, row.shape[-1]))


def pairwise(terms):
    while len(terms) > 1:
        rest = terms[len(terms) // 2 * 2 :]
        terms = [a + b for a, b in zip(terms[::2], terms[1::2])] + rest
    return terms[0]


def lane_block(block):
    return pl.ds(pl.multiple_of(block * LANES, LANES), LANES)


def rows_of(i, half):
    return pl.ds(SUB * i + HALF * half, HALF)


def recur(poles, values):
    last = values[-1]
    sums = [last] * len(poles)
    firsts = None
    for value in values[-2::-1]:
        if firsts is None:
            moved = [p * s for p, s in zip(poles, sums)]
            firsts = moved
        else:
            firsts = [p * (f + s) for p, f, s in zip(poles, firsts, sums)]
            moved = [p * s for p, s in zip(poles, sums)]
        sums = [m + value for m in moved]
    return sums, firsts


def signal_chunk(length, low, high, sig_ref, dec_ref, end_ref, sigp_ref, y_ref, y1_ref, ebuf, e1buf):
    tokens, width = sig_ref.shape[0], high - low
    modes = dec_ref.shape[0]
    steps = tokens // SUB
    sigp_ref[...] = jnp.dot(
        interleave(tokens), sig_ref[:, low:high], preferred_element_type=F32
    ).astype(BF16)

    @pl.loop(0, width // LANES)
    def _(block):
        lanes = lane_block(block)
        there = lane_block(block + low // LANES)
        rate = dec_ref[:, there] * (1.0 / length)
        pole_all = jnp.exp(-rate)
        pole_sub = jnp.exp(-rate * steps)
        both = [sigp_ref[pl.ds(SUB * i, SUB), lanes].astype(F32) for i in range(steps)]
        for half in range(2):
            values = [both[i][HALF * half : HALF * (half + 1)] for i in reversed(range(steps))]
            for first in range(0, modes, 8):
                poles = [spread(pole_all[n : n + 1]) for n in range(first, first + 8)]
                sums, firsts = recur(poles, values)
                for n in range(8):
                    rows = rows_of(first + n, half)
                    end = poles[n] * sums[n]
                    ebuf[rows, :] = end
                    e1buf[rows, :] = poles[n] * firsts[n] + end
        carry = jnp.zeros((modes, LANES), F32)
        carry1 = jnp.zeros((modes, LANES), F32)
        for j in range(SUB):
            pick = pl.ds(j, modes, stride=SUB)
            end, end1 = ebuf[pick, :], e1buf[pick, :]
            ebuf[pick, :] = carry
            e1buf[pick, :] = carry1
            carry1 = pole_sub * (carry1 + steps * carry) + end1
            carry = pole_sub * carry + end
        y_ref[:, lanes] = ebuf[...].astype(BF16)
        y1_ref[:, lanes] = e1buf[...].astype(BF16)
        end_ref[0:modes, there] = carry
        end_ref[modes : 2 * modes, there] = carry1


def gradient_kernel(length, base, lent, parts, *refs):
    own_ref, *got_refs = refs[: 1 + parts]
    (sigp_ref, dec_ref, y_ref, y1_ref,
     grad_ref, z_ref, pay_ref, sbuf, s1buf, rbuf, dbuf, gf) = refs[1 + parts :]
    tokens, width = grad_ref.shape
    modes = dec_ref.shape[0]
    steps = tokens // SUB
    mine = slice(base, base + width)
    place = lax.broadcasted_iota(jnp.int32, (HALF, LANES), 0).astype(F32) * steps
    lent_ref, *got_refs = got_refs
    total = own_ref[:, mine].astype(F32)
    total = total + lent_ref[:, own_ref.shape[1] * lent + base : own_ref.shape[1] * lent + base + width].astype(F32)
    for got in got_refs:
        total = total + got[...].astype(F32)
    grad_ref[...] = jnp.dot(
        interleave(tokens), total.astype(BF16), preferred_element_type=F32
    )

    @pl.loop(0, width // LANES)
    def _(block):
        here = lane_block(block)
        rate = dec_ref[:, lane_block(block + base // LANES)] * (-1.0 / length)
        pole_all = jnp.exp(rate)
        both = [sigp_ref[pl.ds(SUB * i, SUB), here].astype(F32) for i in range(steps)]
        for half in range(2):
            values = [grad_ref[rows_of(i, half), here] for i in range(steps)]
            for first in range(0, modes, 8):
                poles = [spread(pole_all[n : n + 1]) for n in range(first, first + 8)]
                sums, firsts = recur(poles, values)
                for n in range(8):
                    rows = rows_of(first + n, half)
                    out = pl.ds(HALF * (first + n), HALF)
                    before, before1 = y_ref[rows, here].astype(F32), y1_ref[rows, here].astype(F32)
                    reach = jnp.exp(spread(rate[first + n : first + n + 1]) * (place + half * HALF * steps))
                    moved = reach * sums[n]
                    z_ref[block, rows, :] = moved
                    terms = (
                        (sbuf, moved),
                        (s1buf, reach * firsts[n] + (place + half * HALF * steps) * moved),
                        (rbuf, sums[n] * before),
                        (dbuf, sums[n] * before1 + firsts[n] * before),
                    )
                    for ref, term in terms:
                        ref[out, here] = term if half == 0 else ref[out, here] + term
            seen = [v[HALF * half : HALF * (half + 1)] for v in both]
            for lag in range(steps):
                term = pairwise([values[i + lag] * seen[i] for i in range(steps - lag)])
                out = pl.ds(HALF * lag, HALF)
                gf[out, here] = term if half == 0 else gf[out, here] + term

    adder = group_sums(modes, HALF)
    add = lambda m, ref: jnp.dot(m, ref[...], preferred_element_type=F32)
    lags = add(group_sums(steps, HALF), gf)
    res, dec = add(adder, rbuf), add(adder, dbuf)
    state, first = add(adder, sbuf), add(adder, s1buf)
    pole = jnp.exp(dec_ref[:, mine] * (-1.0 / length))
    res = res + lags[0:1]
    weight = pole
    for lag in range(1, steps):
        term = weight * lags[lag : lag + 1]
        res = res + term
        dec = dec + lag * term
        weight = weight * pole
    for k, rows in enumerate((state, res, dec, first)):
        pay_ref[k * modes : (k + 1) * modes, :] = rows
    pay_ref[4 * modes :, :] = jnp.broadcast_to(lags[0:1], (8, width))


def gradient_states(pieces, lent, width, base, sigp, decays, y, y1, length):
    tokens = sigp.shape[0]
    modes = decays.shape[0]
    buf = pltpu.VMEM((modes * HALF, width), F32)
    return pl.pallas_call(
        functools.partial(gradient_kernel, length, base, lent, len(pieces) - 1),
        out_shape=(
            jax.ShapeDtypeStruct((tokens, width), F32),
            jax.ShapeDtypeStruct((width // LANES, modes * SUB, LANES), F32),
            jax.ShapeDtypeStruct((4 * modes + 8, width), F32),
        ),
        in_specs=[VM] * (len(pieces) + 4),
        out_specs=(VM,) * 3,
        scratch_shapes=[buf] * 4 + [pltpu.VMEM((tokens // SUB * HALF, width), F32)],
        compiler_params=params(),
        cost_estimate=SMALL,
        name="gradient_states",
    )(*pieces, sigp, decays, y, y1)


def carry_out(outs, poles, starts):
    outs = list(outs)
    for i in reversed(range(len(outs))):
        outs[i] = outs[i] + pairwise(starts)
        if i:
            starts = [p * s for p, s in zip(poles, starts)]
    return outs


def local_kernel(length, base, grad_ref, z_ref, dec_ref, res_ref, gain_ref, loc_ref, cbuf):
    tokens, width = grad_ref.shape
    modes = dec_ref.shape[0]
    steps = tokens // SUB

    @pl.loop(0, width // LANES)
    def _(block):
        here = lane_block(block)
        lanes = lane_block(block + base // LANES)
        rate = dec_ref[:, lanes] * (1.0 / length)
        pole_all = jnp.exp(-rate)
        weight = res_ref[:, lanes] * (1.0 / math.sqrt(length))
        gain = spread(gain_ref[:, lanes])
        sums = jnp.zeros((modes, LANES), F32)
        for j in reversed(range(SUB)):
            pick = pl.ds(j, modes, stride=SUB)
            back = jnp.exp(rate * (steps * (j + 1) - 1))
            cbuf[pick, :] = weight * (back * sums)
            sums = sums + z_ref[block, pick, :]
        filt = []
        for _ in range(steps):
            filt.append(spread(jnp.sum(weight, axis=0, keepdims=True)))
            weight = weight * pole_all
        for half in range(2):
            values = [grad_ref[rows_of(i, half), here] for i in range(steps)]
            outs = [
                pairwise([filt[lag] * values[i + lag] for lag in range(steps - i)]) for i in range(steps)
            ]
            for first in range(0, modes, 8):
                picked = range(first, first + 8)
                poles = [spread(pole_all[n : n + 1]) for n in picked]
                outs = carry_out(outs, poles, [cbuf[rows_of(n, half), :] for n in picked])
            for i in range(steps):
                loc_ref[rows_of(i, half), here] = outs[i] + gain * values[i]


def local_part(grad, z, decays, residues, gain, length, base):
    tokens, width = grad.shape
    modes = decays.shape[0]
    return pl.pallas_call(
        functools.partial(local_kernel, length, base),
        out_shape=jax.ShapeDtypeStruct((tokens, width), F32),
        in_specs=[VM] * 5,
        out_specs=VM,
        scratch_shapes=[pltpu.VMEM((modes * SUB, LANES), F32)],
        compiler_params=params(),
        cost_estimate=SMALL,
        name="local_part",
    )(grad, z, decays, residues, gain)


def finish_kernel(length, hop, chunks, me_ref, there_ref, state_ref, later_ref, dec_ref, res_ref, *refs):
    locs = refs[: len(chunks)]
    o_ref, ores_ref, odec_ref, oskip_ref, vals = refs[len(chunks) :]
    tokens = o_ref.shape[0]
    modes = dec_ref.shape[0]
    steps = tokens // SUB
    scale = 1.0 / math.sqrt(length)
    ahead = (SUB - 1 - lax.broadcasted_iota(jnp.int32, (HALF, LANES), 0)).astype(F32) * steps
    vals[...] = later_step(me_ref, there_ref, later_ref, dec_ref, length, tokens, hop)

    for loc_ref, (low, high) in zip(locs, chunks):
        @pl.loop(0, (high - low) // LANES)
        def _(block):
            here = lane_block(block)
            lanes = lane_block(block + low // LANES)
            rate = dec_ref[:, lanes] * (-1.0 / length)
            pole_all = jnp.exp(rate)
            lead = scale * res_ref[:, lanes] * pole_all * vals[:, lanes]
            for half in range(2):
                outs = [loc_ref[rows_of(i, half), here] for i in range(steps)]
                for first in range(0, modes, 8):
                    picked = range(first, first + 8)
                    poles = [spread(pole_all[n : n + 1]) for n in picked]
                    starts = [
                        spread(lead[n : n + 1]) * jnp.exp(spread(rate[n : n + 1]) * (ahead - half * HALF * steps))
                        for n in picked
                    ]
                    outs = carry_out(outs, poles, starts)
                for i in range(steps):
                    loc_ref[rows_of(i, half), here] = outs[i]

    turn = interleave(tokens, transpose=True)
    for loc_ref, (low, high) in zip(locs, chunks):
        o_ref[:, low:high] = jnp.dot(
            turn, loc_ref[...].astype(BF16), preferred_element_type=F32
        ).astype(BF16)
    sums = state_ref[modes:, :] + there_ref[modes:, :].astype(F32)
    ores_ref[...] = sums[0:modes] * (1.0 / length)
    odec_ref[...] = sums[modes : 2 * modes] * (-1.0 / (length * length)) * res_ref[...]
    oskip_ref[...] = sums[2 * modes : 2 * modes + 1] * scale


def finish(me, there, state, later, decays, residues, locs, chunks, tokens, length, hop):
    modes, width = decays.shape
    return pl.pallas_call(
        functools.partial(finish_kernel, length, hop, chunks),
        out_shape=(
            jax.ShapeDtypeStruct((tokens, width), BF16),
            jax.ShapeDtypeStruct((modes, width), F32),
            jax.ShapeDtypeStruct((modes, width), F32),
            jax.ShapeDtypeStruct((1, width), F32),
        ),
        in_specs=[SM] + [VM] * (5 + len(locs)),
        out_specs=(VM,) * 4,
        scratch_shapes=[pltpu.VMEM((modes, width), F32)],
        compiler_params=params(),
        cost_estimate=SMALL,
        name="finish",
    )(me, there, state, later, decays, residues, *locs)


def place_bits(me_ref, hop):
    me = me_ref[0]
    return (me & (hop - 1)).astype(F32), (me & hop) != 0


def prefix_kernel(length, tokens, hop, me_ref, there_ref, state_ref, *refs):
    *before_ref, dec_ref, sent_ref, next_ref, after_ref = refs
    modes = dec_ref.shape[0]
    rate = dec_ref[...] * (1.0 / length)
    there = there_ref[...].astype(F32)
    other, other1 = there[:modes], there[modes:]
    state, first = state_ref[0:modes, :], state_ref[modes : 2 * modes, :]
    inside, upper = place_bits(me_ref, hop)
    reach = jnp.exp(-rate * (inside * tokens))
    after = jnp.where(upper, reach * other, 0.0)
    after1 = jnp.where(upper, reach * (other1 + (inside * tokens) * other), 0.0)
    if before_ref:
        after = after + before_ref[0][0:modes, :]
        after1 = after1 + before_ref[0][modes : 2 * modes, :]
    after_ref[0:modes, :] = after
    after_ref[modes : 2 * modes, :] = after1
    span = jnp.exp(-rate * (hop * tokens))
    late, early = jnp.where(upper, state, other), jnp.where(upper, other, state)
    late1, early1 = jnp.where(upper, first, other1), jnp.where(upper, other1, first)
    first = late1 + span * (early1 + (hop * tokens) * early)
    state = late + span * early
    for rows, value in ((slice(0, modes), state), (slice(modes, 2 * modes), first)):
        next_ref[rows, :] = value
        sent_ref[rows, :] = value.astype(BF16)


def later_step(me_ref, there_ref, later_ref, dec_ref, length, tokens, hop):
    modes = dec_ref.shape[0]
    inside, upper = place_bits(me_ref, hop)
    reach = jnp.exp(dec_ref[...] * (-1.0 / length) * ((hop - 1 - inside) * tokens))
    return later_ref[...] + jnp.where(upper, 0.0, reach * there_ref[0:modes, :].astype(F32))


def suffix_kernel(length, tokens, hop, me_ref, there_ref, state_ref, later_ref, dec_ref, sent_ref, next_ref, after_ref):
    modes = dec_ref.shape[0]
    after_ref[...] = later_step(me_ref, there_ref, later_ref, dec_ref, length, tokens, hop)
    _, upper = place_bits(me_ref, hop)
    span = jnp.exp(dec_ref[...] * (-1.0 / length) * (hop * tokens))
    there = there_ref[...].astype(F32)
    state, other = state_ref[0:modes, :], there[:modes]
    state = jnp.where(upper, other, state) + span * jnp.where(upper, state, other)
    sums = state_ref[modes:, :] + there[modes:]
    next_ref[0:modes, :] = state
    next_ref[modes:, :] = sums
    sent_ref[0:modes, :] = state.astype(BF16)
    sent_ref[modes:, :] = sums.astype(BF16)


def step_call(kernel, me, there, state, carried, decays):
    rows = state.shape[0] if kernel.func is prefix_kernel else decays.shape[0]
    args = [there, state, *carried, decays]
    return pl.pallas_call(
        kernel,
        out_shape=(
            jax.ShapeDtypeStruct(state.shape, BF16),
            jax.ShapeDtypeStruct(state.shape, F32),
            jax.ShapeDtypeStruct((rows, decays.shape[1]), F32),
        ),
        in_specs=[SM] + [VM] * len(args),
        out_specs=(VM,) * 3,
        compiler_params=params(),
        cost_estimate=SMALL,
        name="exchange_step",
    )(me, *args)


def gather_kernel(chunks, modes, before_ref, *refs):
    pays, (sent_ref, state_ref, later_ref) = refs[: len(chunks)], refs[len(chunks) :]
    later_ref[...] = jnp.zeros_like(later_ref)
    for pay_ref, (low, high) in zip(pays, chunks):
        state, res, dec, first = [pay_ref[k * modes : (k + 1) * modes, :] for k in range(4)]
        before = before_ref[0:modes, low:high]
        before1 = before_ref[modes : 2 * modes, low:high]
        res = res + state * before
        dec = dec + first * before + state * before1
        for k, value in enumerate((state, res, dec, pay_ref[4 * modes :, :])):
            rows = slice(k * modes, k * modes + value.shape[0])
            state_ref[rows, low:high] = value
            sent_ref[rows, low:high] = value.astype(BF16)


def gather_sums(pays, before, chunks):
    modes, width = before.shape[0] // 2, before.shape[1]
    rows = pays[0].shape[0] - modes
    return pl.pallas_call(
        functools.partial(gather_kernel, chunks, modes),
        out_shape=(
            jax.ShapeDtypeStruct((rows, width), BF16),
            jax.ShapeDtypeStruct((rows, width), F32),
            jax.ShapeDtypeStruct((modes, width), F32),
        ),
        in_specs=[VM] * (1 + len(pays)),
        out_specs=(VM,) * 3,
        compiler_params=params(),
        cost_estimate=SMALL,
        name="gather_sums",
    )(before, *pays)


def start_weights(blocks_ref, w_ref, w_buf, sems):
    width = w_buf.shape[1]
    copies = []
    for q in range(w_buf.shape[0]):
        start = pl.multiple_of(blocks_ref[q] * width, width)
        copies.append(pltpu.make_async_copy(w_ref.at[pl.ds(start, width)], w_buf.at[q], sems.at[q]))
        copies[-1].start()
    return copies


def finish_weights(copies, up_ref, w_buf, outs):
    width = w_buf.shape[1]
    for copy in copies:
        copy.wait()
    rows = min(width, 256)
    for q, out in enumerate(outs):
        for start in range(0, width, rows):
            out[:, start : start + rows] = lax.dot_general(
                up_ref[...], w_buf[q, start : start + rows, :], (((1,), (1,)), ((), ())),
                preferred_element_type=F32,
            ).astype(out.dtype)


def project_kernel(pieces, blocks_ref, up_ref, w_ref, *refs):
    outs, (w_buf, sems) = refs[:pieces], refs[pieces:]
    finish_weights(start_weights(blocks_ref, w_ref, w_buf, sems), up_ref, w_buf, outs)


def first_kernel(pieces, chunks, length, blocks_ref, up_ref, w_ref, sig_ref, dec_ref, *refs):
    lents = pieces // 2 + 1
    lent_ref, *pairs = refs[:lents]
    end_ref, sent_ref, *tables = refs[lents:-4]
    w_buf, sems, ebuf, e1buf = refs[-4:]
    width = w_buf.shape[1]
    outs = [lent_ref.at[:, k * width : (k + 1) * width] for k in range(lents)] + pairs
    copies = start_weights(blocks_ref, w_ref, w_buf, sems)
    for k, (low, high) in enumerate(chunks):
        signal_chunk(length, low, high, sig_ref, dec_ref, end_ref, *tables[3 * k : 3 * k + 3], ebuf, e1buf)
    sent_ref[...] = end_ref[...].astype(BF16)
    finish_weights(copies, up_ref, w_buf, outs)


def weight_scratch(pieces, width, feats):
    return [pltpu.VMEM((pieces, width, feats), BF16), pltpu.SemaphoreType.DMA((pieces,))]


def project(up, weight, width, blocks):
    tokens, feats = up.shape
    pieces = len(blocks)
    return pl.pallas_call(
        functools.partial(project_kernel, pieces),
        out_shape=[jax.ShapeDtypeStruct((tokens, width), BF16)] * pieces,
        in_specs=[pl.BlockSpec(memory_space=pltpu.SMEM), VM, pl.BlockSpec(memory_space=pl.ANY)],
        out_specs=[VM] * pieces,
        scratch_shapes=weight_scratch(pieces, width, feats),
        compiler_params=params(PROJECT_LIMIT),
        cost_estimate=SMALL,
        name="project",
    )(jnp.stack(blocks).astype(jnp.int32), up, weight)


def project_and_scan(up, weight, width, blocks, signal, decays, chunks, length):
    tokens, feats = up.shape
    modes = decays.shape[0]
    pieces = len(blocks)
    lents = pieces // 2 + 1
    shapes = [jax.ShapeDtypeStruct((tokens, lents * width), BF16)]
    shapes += [jax.ShapeDtypeStruct((tokens, width), BF16)] * (pieces - lents)
    shapes += [jax.ShapeDtypeStruct((2 * modes, width), dtype) for dtype in (F32, BF16)]
    for low, high in chunks:
        states = jax.ShapeDtypeStruct((modes * SUB, high - low), BF16)
        shapes += [jax.ShapeDtypeStruct((tokens, high - low), BF16), states, states]
    out = pl.pallas_call(
        functools.partial(first_kernel, pieces, chunks, length),
        out_shape=shapes,
        in_specs=[pl.BlockSpec(memory_space=pltpu.SMEM), VM, pl.BlockSpec(memory_space=pl.ANY), VM, VM],
        out_specs=[VM] * len(shapes),
        scratch_shapes=weight_scratch(pieces, width, feats) + [pltpu.VMEM((modes * SUB, LANES), F32)] * 2,
        compiler_params=params(PROJECT_LIMIT),
        cost_estimate=SMALL,
        name="project_and_scan",
    )(jnp.stack(blocks).astype(jnp.int32), up, weight, signal, decays)
    start = 1 + pieces - lents
    tables = out[start + 2 :]
    return out[0], out[1:start], out[start : start + 2], [
        tables[3 * k : 3 * k + 3] for k in range(len(chunks))
    ]


def pair_kernel(chunks, lent, mine_ref, lent_ref, *outs):
    base = mine_ref.shape[1] * lent
    for (low, high), out in zip(chunks, outs):
        total = mine_ref[:, low:high].astype(F32) + lent_ref[:, base + low : base + high].astype(F32)
        out[...] = total.astype(BF16)


def pair_sums(mine, lent, index, chunks):
    tokens = mine.shape[0]
    return pl.pallas_call(
        functools.partial(pair_kernel, chunks, index),
        out_shape=[jax.ShapeDtypeStruct((tokens, high - low), BF16) for low, high in chunks],
        in_specs=[VM] * 2,
        out_specs=[VM] * len(chunks),
        compiler_params=params(),
        cost_estimate=SMALL,
        name="pair_sums",
    )(mine, lent)


def send(x, axis, size, hop):
    return lax.ppermute(x, axis, [(i, i ^ hop) for i in range(size)])


def cuts(width):
    lane_blocks = width // LANES
    first = lane_blocks // 2 * LANES
    return [(0, first), (first, width)]


def body(signal, upstream, out_weight, residues, decays, skip_gain):
    tokens, width = signal.shape
    groups = lax.axis_size("ctx")
    blocks = lax.axis_size("ch")
    length = tokens * groups
    modes = residues.shape[1]
    me = lax.axis_index("ch")
    place = jnp.reshape(lax.axis_index("ctx").astype(jnp.int32), (1,))
    dec = decays.T
    res = residues.T
    gain = skip_gain[None, :]
    chunks = cuts(width)
    hops = range(2, blocks, 2)
    levels = [1 << k for k in range(groups.bit_length() - 1)]

    wanted = [me ^ hop ^ 1 for hop in hops] + [me ^ 1] + [me ^ hop for hop in hops]
    lent, parts, (state, sent), tables = project_and_scan(
        upstream, out_weight, width, wanted, signal, dec, chunks, length
    )
    lent = send(lent, "ch", blocks, 1)
    pairs = [pair_sums(part, lent, index, chunks) for index, part in enumerate(parts)]
    upstream, pairs = lax.optimization_barrier((upstream, pairs))
    arrived = [[send(pair[k], "ch", blocks, hop) for pair, hop in zip(pairs, hops)] for k in range(len(chunks))]
    (own,) = project(upstream, out_weight, width, [me])

    before = []
    for hop in levels:
        if hop == levels[-1]:
            sent, arrived = lax.optimization_barrier((sent, arrived))
        there = send(sent, "ctx", groups, hop)
        sent, state, *before = step_call(
            functools.partial(prefix_kernel, length, tokens, hop), place, there, state, before, dec
        )
    pays, locs = [], []
    for chunk, (low, high), (sigp, y, y1) in zip(arrived, chunks, tables):
        grad, z, pay = gradient_states(
            [own, lent, *chunk], len(hops), high - low, low, sigp, dec, y, y1, length
        )
        pays.append(pay)
        locs.append((grad, z, low))
    sent, state, later = gather_sums(pays, before[0], chunks)
    locs = [local_part(grad, z, dec, res, gain, length, low) for grad, z, low in locs]
    for hop in levels[:-1]:
        there = send(sent, "ctx", groups, hop)
        sent, state, later = step_call(
            functools.partial(suffix_kernel, length, tokens, hop), place, there, state, [later], dec
        )
    there = send(sent, "ctx", groups, levels[-1])
    out, ores, odec, oskip = finish(
        place, there, state, later, dec, res, locs, chunks, tokens, length, levels[-1]
    )
    return (out, ores.T, odec.T, oskip[0])


def solution(mesh):
    placed = (P("ctx", "ch"), P("ctx", "ch"), P(None, "ch"), P("ch", None), P("ch", None), P("ch"))
    return jax.shard_map(
        body,
        mesh=mesh,
        in_specs=placed,
        out_specs=(P("ctx", "ch"), P("ch", None), P("ch", None), P("ch")),
        check_vma=False,
    )
```

```python
import functools
import math

import jax
import jax.numpy as jnp
from jax import lax
from jax.experimental import pallas as pl
from jax.experimental.pallas import tpu as pltpu
from jax.sharding import PartitionSpec as P

F32 = jnp.float32
BF16 = jnp.bfloat16
SUB = 16
HALF = 8
LANES = 128
VMEM_LIMIT = 12 * 1024 * 1024
PROJECT_LIMIT = 43 * 1024 * 1024
VM = pl.BlockSpec(memory_space=pltpu.VMEM)
SM = pl.BlockSpec(memory_space=pltpu.SMEM)


def interleave(tokens, transpose=False):
    steps = tokens // SUB
    row = lax.broadcasted_iota(jnp.int32, (tokens, tokens), 1 if transpose else 0)
    col = lax.broadcasted_iota(jnp.int32, (tokens, tokens), 0 if transpose else 1)
    return jnp.where(col == (row % SUB) * steps + row // SUB, 1.0, 0.0).astype(BF16)


def group_sums(groups, size):
    col = lax.broadcasted_iota(jnp.int32, (groups, groups * size), 1)
    row = lax.broadcasted_iota(jnp.int32, (groups, groups * size), 0)
    return jnp.where(col // size == row, 1.0, 0.0).astype(F32)


def params(limit=VMEM_LIMIT):
    return pltpu.CompilerParams(vmem_limit_bytes=limit)


SMALL = pl.CostEstimate(flops=1, bytes_accessed=1, transcendentals=0)


def takes(microseconds):
    return pl.CostEstimate(flops=int(microseconds * 1e9), bytes_accessed=1, transcendentals=0)


def spread(row):
    return jnp.broadcast_to(row, (HALF, row.shape[-1]))


def pairwise(terms):
    while len(terms) > 1:
        rest = terms[len(terms) // 2 * 2 :]
        terms = [a + b for a, b in zip(terms[::2], terms[1::2])] + rest
    return terms[0]


def lane_block(block):
    return pl.ds(pl.multiple_of(block * LANES, LANES), LANES)


def rows_of(i, half):
    return pl.ds(SUB * i + HALF * half, HALF)


def recur(poles, values):
    last = values[-1]
    sums = [last] * len(poles)
    firsts = None
    for value in values[-2::-1]:
        if firsts is None:
            moved = [p * s for p, s in zip(poles, sums)]
            firsts = moved
        else:
            firsts = [p * (f + s) for p, f, s in zip(poles, firsts, sums)]
            moved = [p * s for p, s in zip(poles, sums)]
        sums = [m + value for m in moved]
    return sums, firsts


def signal_chunk(length, low, high, sig_ref, dec_ref, end_ref, sigp_ref, y_ref, y1_ref, ebuf, e1buf):
    tokens, width = sig_ref.shape[0], high - low
    modes = dec_ref.shape[0]
    steps = tokens // SUB
    sigp_ref[...] = jnp.dot(
        interleave(tokens), sig_ref[:, low:high], preferred_element_type=F32
    ).astype(BF16)

    @pl.loop(0, width // LANES)
    def _(block):
        lanes = lane_block(block)
        there = lane_block(block + low // LANES)
        rate = dec_ref[:, there] * (1.0 / length)
        pole_all = jnp.exp(-rate)
        pole_sub = jnp.exp(-rate * steps)
        both = [sigp_ref[pl.ds(SUB * i, SUB), lanes].astype(F32) for i in range(steps)]
        for half in range(2):
            values = [both[i][HALF * half : HALF * (half + 1)] for i in reversed(range(steps))]
            for first in range(0, modes, 8):
                poles = [spread(pole_all[n : n + 1]) for n in range(first, first + 8)]
                sums, firsts = recur(poles, values)
                for n in range(8):
                    rows = rows_of(first + n, half)
                    end = poles[n] * sums[n]
                    ebuf[rows, :] = end
                    e1buf[rows, :] = poles[n] * firsts[n] + end
        carry = jnp.zeros((modes, LANES), F32)
        carry1 = jnp.zeros((modes, LANES), F32)
        for j in range(SUB):
            pick = pl.ds(j, modes, stride=SUB)
            end, end1 = ebuf[pick, :], e1buf[pick, :]
            ebuf[pick, :] = carry
            e1buf[pick, :] = carry1
            carry1 = pole_sub * (carry1 + steps * carry) + end1
            carry = pole_sub * carry + end
        y_ref[:, lanes] = ebuf[...].astype(BF16)
        y1_ref[:, lanes] = e1buf[...].astype(BF16)
        end_ref[0:modes, there] = carry
        end_ref[modes : 2 * modes, there] = carry1


def gradient_kernel(length, base, lent, parts, *refs):
    own_ref, lent_ref, *got_refs = refs[: 1 + parts]
    dec_ref, grad_ref, z_ref, state_ref, sbuf = refs[1 + parts :]
    tokens, width = grad_ref.shape
    modes = dec_ref.shape[0]
    steps = tokens // SUB
    first_lent = own_ref.shape[1] * lent + base
    place = lax.broadcasted_iota(jnp.int32, (HALF, LANES), 0).astype(F32) * steps
    total = own_ref[:, base : base + width].astype(F32)
    total = total + lent_ref[:, first_lent : first_lent + width].astype(F32)
    for got in got_refs:
        total = total + got[...].astype(F32)
    grad_ref[...] = jnp.dot(
        interleave(tokens), total.astype(BF16), preferred_element_type=F32
    )

    @pl.loop(0, width // LANES)
    def _(block):
        here = lane_block(block)
        rate = dec_ref[:, lane_block(block + base // LANES)] * (-1.0 / length)
        pole_all = jnp.exp(rate)
        for half in range(2):
            values = [grad_ref[rows_of(i, half), here] for i in range(steps)]
            for first in range(0, modes, 8):
                poles = [spread(pole_all[n : n + 1]) for n in range(first, first + 8)]
                sums = [values[-1]] * 8
                for value in values[-2::-1]:
                    sums = [p * v + value for p, v in zip(poles, sums)]
                for n in range(8):
                    out = pl.ds(HALF * (first + n), HALF)
                    reach = jnp.exp(spread(rate[first + n : first + n + 1]) * (place + half * HALF * steps))
                    moved = reach * sums[n]
                    z_ref[block, rows_of(first + n, half), :] = moved
                    sbuf[out, here] = moved if half == 0 else sbuf[out, here] + moved

    state_ref[...] = jnp.dot(group_sums(modes, HALF), sbuf[...], preferred_element_type=F32)


def gradient_states(pieces, lent, width, base, decays, length):
    tokens = pieces[0].shape[0]
    modes = decays.shape[0]
    return pl.pallas_call(
        functools.partial(gradient_kernel, length, base, lent, len(pieces) - 1),
        out_shape=(
            jax.ShapeDtypeStruct((tokens, width), F32),
            jax.ShapeDtypeStruct((width // LANES, modes * SUB, LANES), F32),
            jax.ShapeDtypeStruct((modes, width), F32),
        ),
        in_specs=[VM] * (len(pieces) + 1),
        out_specs=(VM,) * 3,
        scratch_shapes=[pltpu.VMEM((modes * HALF, width), F32)],
        compiler_params=params(),
        cost_estimate=takes(1),
        name="gradient_states",
    )(*pieces, decays)


def filter_kernel(length, base, grad_ref, sigp_ref, dec_ref, y_ref, y1_ref, pay_ref, s1buf, rbuf, dbuf, gf):
    tokens, width = grad_ref.shape
    modes = dec_ref.shape[0]
    steps = tokens // SUB
    place = lax.broadcasted_iota(jnp.int32, (HALF, LANES), 0).astype(F32) * steps

    @pl.loop(0, width // LANES)
    def _(block):
        here = lane_block(block)
        rate = dec_ref[:, lane_block(block + base // LANES)] * (-1.0 / length)
        pole_all = jnp.exp(rate)
        both = [sigp_ref[pl.ds(SUB * i, SUB), here].astype(F32) for i in range(steps)]
        for half in range(2):
            values = [grad_ref[rows_of(i, half), here] for i in range(steps)]
            for first in range(0, modes, 8):
                poles = [spread(pole_all[n : n + 1]) for n in range(first, first + 8)]
                sums, firsts = recur(poles, values)
                for n in range(8):
                    rows = rows_of(first + n, half)
                    out = pl.ds(HALF * (first + n), HALF)
                    before, before1 = y_ref[rows, here].astype(F32), y1_ref[rows, here].astype(F32)
                    ahead = place + half * HALF * steps
                    reach = jnp.exp(spread(rate[first + n : first + n + 1]) * ahead)
                    terms = (
                        (s1buf, reach * (firsts[n] + ahead * sums[n])),
                        (rbuf, sums[n] * before),
                        (dbuf, sums[n] * before1 + firsts[n] * before),
                    )
                    for ref, term in terms:
                        ref[out, here] = term if half == 0 else ref[out, here] + term
            seen = [v[HALF * half : HALF * (half + 1)] for v in both]
            for lag in range(steps):
                term = pairwise([values[i + lag] * seen[i] for i in range(steps - lag)])
                out = pl.ds(HALF * lag, HALF)
                gf[out, here] = term if half == 0 else gf[out, here] + term

    adder = group_sums(modes, HALF)
    add = lambda m, ref: jnp.dot(m, ref[...], preferred_element_type=F32)
    lags = add(group_sums(steps, HALF), gf)
    res, dec, first = add(adder, rbuf), add(adder, dbuf), add(adder, s1buf)
    pole = jnp.exp(dec_ref[:, base : base + width] * (-1.0 / length))
    res = res + lags[0:1]
    weight = pole
    for lag in range(1, steps):
        term = weight * lags[lag : lag + 1]
        res = res + term
        dec = dec + lag * term
        weight = weight * pole
    for k, rows in enumerate((res, dec, first, jnp.broadcast_to(lags[0:1], (modes, width)))):
        pay_ref[k * modes : (k + 1) * modes, :] = rows


def filter_sums(grad, sigp, decays, y, y1, length, base):
    tokens, width = grad.shape
    modes = decays.shape[0]
    buf = pltpu.VMEM((modes * HALF, width), F32)
    return pl.pallas_call(
        functools.partial(filter_kernel, length, base),
        out_shape=jax.ShapeDtypeStruct((4 * modes, width), F32),
        in_specs=[VM] * 5,
        out_specs=VM,
        scratch_shapes=[buf] * 3 + [pltpu.VMEM((tokens // SUB * HALF, width), F32)],
        compiler_params=params(),
        cost_estimate=takes(3),
        name="filter_sums",
    )(grad, sigp, decays, y, y1)


def carry_out(outs, poles, starts):
    outs = list(outs)
    for i in reversed(range(len(outs))):
        outs[i] = outs[i] + pairwise(starts)
        if i:
            starts = [p * s for p, s in zip(poles, starts)]
    return outs


def local_kernel(length, base, grad_ref, z_ref, dec_ref, res_ref, gain_ref, loc_ref, cbuf):
    tokens, width = grad_ref.shape
    modes = dec_ref.shape[0]
    steps = tokens // SUB

    @pl.loop(0, width // LANES)
    def _(block):
        here = lane_block(block)
        lanes = lane_block(block + base // LANES)
        rate = dec_ref[:, lanes] * (1.0 / length)
        pole_all = jnp.exp(-rate)
        weight = res_ref[:, lanes] * (1.0 / math.sqrt(length))
        gain = spread(gain_ref[:, lanes])
        sums = jnp.zeros((modes, LANES), F32)
        for j in reversed(range(SUB)):
            pick = pl.ds(j, modes, stride=SUB)
            back = jnp.exp(rate * (steps * (j + 1) - 1))
            cbuf[pick, :] = weight * (back * sums)
            sums = sums + z_ref[block, pick, :]
        filt = []
        for _ in range(steps):
            filt.append(spread(jnp.sum(weight, axis=0, keepdims=True)))
            weight = weight * pole_all
        for half in range(2):
            values = [grad_ref[rows_of(i, half), here] for i in range(steps)]
            outs = [
                pairwise([filt[lag] * values[i + lag] for lag in range(steps - i)]) for i in range(steps)
            ]
            for first in range(0, modes, 8):
                picked = range(first, first + 8)
                poles = [spread(pole_all[n : n + 1]) for n in picked]
                outs = carry_out(outs, poles, [cbuf[rows_of(n, half), :] for n in picked])
            for i in range(steps):
                loc_ref[rows_of(i, half), here] = outs[i] + gain * values[i]


def local_part(grad, z, decays, residues, gain, length, base):
    tokens, width = grad.shape
    modes = decays.shape[0]
    return pl.pallas_call(
        functools.partial(local_kernel, length, base),
        out_shape=jax.ShapeDtypeStruct((tokens, width), F32),
        in_specs=[VM] * 5,
        out_specs=VM,
        scratch_shapes=[pltpu.VMEM((modes * SUB, LANES), F32)],
        compiler_params=params(),
        cost_estimate=takes(1.5),
        name="local_part",
    )(grad, z, decays, residues, gain)


def finish_kernel(length, hop, chunks, me_ref, there_ref, later_ref, dec_ref, res_ref, *refs):
    locs = refs[: len(chunks)]
    o_ref, vals = refs[len(chunks) :]
    tokens = o_ref.shape[0]
    modes = dec_ref.shape[0]
    steps = tokens // SUB
    scale = 1.0 / math.sqrt(length)
    ahead = (SUB - 1 - lax.broadcasted_iota(jnp.int32, (HALF, LANES), 0)).astype(F32) * steps
    vals[...] = later_step(
        me_ref, there_ref.at[0:modes, :], later_ref[...], dec_ref, length, tokens, hop
    )

    for loc_ref, (low, high) in zip(locs, chunks):
        @pl.loop(0, (high - low) // LANES)
        def _(block):
            here = lane_block(block)
            lanes = lane_block(block + low // LANES)
            rate = dec_ref[:, lanes] * (-1.0 / length)
            pole_all = jnp.exp(rate)
            lead = scale * res_ref[:, lanes] * pole_all * vals[:, lanes]
            for half in range(2):
                outs = [loc_ref[rows_of(i, half), here] for i in range(steps)]
                for first in range(0, modes, 8):
                    picked = range(first, first + 8)
                    poles = [spread(pole_all[n : n + 1]) for n in picked]
                    starts = [
                        spread(lead[n : n + 1]) * jnp.exp(spread(rate[n : n + 1]) * (ahead - half * HALF * steps))
                        for n in picked
                    ]
                    outs = carry_out(outs, poles, starts)
                for i in range(steps):
                    loc_ref[rows_of(i, half), here] = outs[i]

    turn = interleave(tokens, transpose=True)
    for loc_ref, (low, high) in zip(locs, chunks):
        o_ref[:, low:high] = jnp.dot(
            turn, loc_ref[...].astype(BF16), preferred_element_type=F32
        ).astype(BF16)


def finish(me, there, later, decays, residues, locs, chunks, tokens, length, hop):
    modes, width = decays.shape
    return pl.pallas_call(
        functools.partial(finish_kernel, length, hop, chunks),
        out_shape=jax.ShapeDtypeStruct((tokens, width), BF16),
        in_specs=[SM] + [VM] * (4 + len(locs)),
        out_specs=VM,
        scratch_shapes=[pltpu.VMEM((modes, width), F32)],
        compiler_params=params(),
        cost_estimate=takes(3),
        name="finish",
    )(me, there, later, decays, residues, *locs)


def place_bits(me_ref, hop):
    me = me_ref[0]
    return (me & (hop - 1)).astype(F32), (me & hop) != 0


def before_step(me_ref, there_ref, before_refs, dec_ref, length, tokens, hop):
    modes = dec_ref.shape[0]
    inside, upper = place_bits(me_ref, hop)
    reach = jnp.exp(dec_ref[...] * (-1.0 / length) * (inside * tokens))
    other, other1 = there_ref[0:modes, :].astype(F32), there_ref[modes : 2 * modes, :].astype(F32)
    before = jnp.where(upper, reach * other, 0.0)
    before1 = jnp.where(upper, reach * (other1 + (inside * tokens) * other), 0.0)
    for ref in before_refs:
        before = before + ref[0:modes, :]
        before1 = before1 + ref[modes : 2 * modes, :]
    return before, before1


def prefix_kernel(length, tokens, hop, carried, me_ref, there_ref, state_ref, *refs):
    refs, (sent_ref, after_ref, *next_ref) = refs[: 1 + carried], refs[1 + carried :]
    *before_refs, dec_ref = refs
    modes = dec_ref.shape[0]
    rows, rows1 = slice(0, modes), slice(modes, 2 * modes)
    after_ref[rows, :], after_ref[rows1, :] = before_step(
        me_ref, there_ref, before_refs, dec_ref, length, tokens, hop
    )
    other, other1 = there_ref[rows, :].astype(F32), there_ref[rows1, :].astype(F32)
    state, first = state_ref[rows, :], state_ref[rows1, :]
    _, upper = place_bits(me_ref, hop)
    span = jnp.exp(dec_ref[...] * (-1.0 / length) * (hop * tokens))
    late, early = jnp.where(upper, state, other), jnp.where(upper, other, state)
    late1, early1 = jnp.where(upper, first, other1), jnp.where(upper, other1, first)
    first = late1 + span * (early1 + (hop * tokens) * early)
    state = late + span * early
    for part, value in ((rows, state), (rows1, first)):
        for ref in next_ref:
            ref[part, :] = value
        sent_ref[part, :] = value.astype(BF16)


def later_step(me_ref, there_ref, later, dec_ref, length, tokens, hop):
    inside, upper = place_bits(me_ref, hop)
    reach = jnp.exp(dec_ref[...] * (-1.0 / length) * ((hop - 1 - inside) * tokens))
    return later + jnp.where(upper, 0.0, reach * there_ref[...].astype(F32))


def suffix_step(me_ref, other, state, dec_ref, length, tokens, hop):
    _, upper = place_bits(me_ref, hop)
    span = jnp.exp(dec_ref[...] * (-1.0 / length) * (hop * tokens))
    return jnp.where(upper, other, state) + span * jnp.where(upper, state, other)


def merge_kernel(
    length, tokens, hop, last, chunks, me_ref, there_ref, state_ref, ends_ref, *refs
):
    sent_ref, next_ref, later_ref, sums_ref = refs[-4:]
    pays, (dec_ref, *before_refs) = refs[: len(chunks)], refs[len(chunks) : -4]
    modes = dec_ref.shape[0]
    all_before, all_before1 = before_step(me_ref, ends_ref, before_refs, dec_ref, length, tokens, last)
    nothing = jnp.zeros_like(later_ref)
    later_ref[...] = later_step(me_ref, there_ref, nothing, dec_ref, length, tokens, hop)
    state = suffix_step(
        me_ref, there_ref[...].astype(F32), state_ref[...], dec_ref, length, tokens, hop
    )
    next_ref[...] = state
    sent_ref[0:modes, :] = state.astype(BF16)
    for pay_ref, (low, high) in zip(pays, chunks):
        res, dec, first, skip = [pay_ref[k * modes : (k + 1) * modes, :] for k in range(4)]
        before, before1 = all_before[:, low:high], all_before1[:, low:high]
        start = state_ref[:, low:high]
        res = res + start * before
        dec = dec + first * before + start * before1
        for k, value in enumerate((res, dec, skip)):
            sums_ref[k * modes : (k + 1) * modes, low:high] = value
            sent_ref[(k + 1) * modes : (k + 2) * modes, low:high] = value.astype(BF16)


def merge(me, there, state, ends, pays, decays, before, chunks, tokens, length, hop, last):
    modes, width = decays.shape
    args = (there, state, ends, *pays, decays, *before)
    return pl.pallas_call(
        functools.partial(merge_kernel, length, tokens, hop, last, chunks),
        out_shape=tuple(
            jax.ShapeDtypeStruct((k * modes, width), dtype)
            for k, dtype in ((4, BF16), (1, F32), (1, F32), (3, F32))
        ),
        in_specs=[SM] + [VM] * len(args),
        out_specs=(VM,) * 4,
        compiler_params=params(),
        cost_estimate=SMALL,
        name="merge",
    )(me, *args)


def tail_kernel(
    length, tokens, hop, me_ref, there_ref, state_ref, later_ref, sums_ref, dec_ref,
    sent_ref, after_ref, total_ref, *next_ref,
):
    modes = dec_ref.shape[0]
    there = there_ref.at[0:modes, :]
    after_ref[...] = later_step(me_ref, there, later_ref[...], dec_ref, length, tokens, hop)
    state = suffix_step(me_ref, there[...].astype(F32), state_ref[...], dec_ref, length, tokens, hop)
    if next_ref:
        next_ref[0][...] = state
    sent_ref[0:modes, :] = state.astype(BF16)
    sums = sums_ref[...] + there_ref[modes:, :].astype(F32)
    total_ref[...] = sums
    sent_ref[modes:, :] = sums.astype(BF16)


def tail_step(me, there, state, later, sums, decays, tokens, length, hop, more):
    args = (there, state, later, sums, decays)
    outs = (there, later, sums) + ((state,) if more else ())
    return pl.pallas_call(
        functools.partial(tail_kernel, length, tokens, hop),
        out_shape=tuple(jax.ShapeDtypeStruct(x.shape, x.dtype) for x in outs),
        in_specs=[SM] + [VM] * 5,
        out_specs=(VM,) * len(outs),
        compiler_params=params(),
        cost_estimate=SMALL,
        name="tail_step",
    )(me, *args)


def sum_kernel(there_ref, sums_ref, sent_ref, total_ref):
    sums = sums_ref[...] + there_ref[there_ref.shape[0] - sums_ref.shape[0] :, :].astype(F32)
    total_ref[...] = sums
    sent_ref[...] = sums.astype(BF16)


def sum_step(there, sums):
    return pl.pallas_call(
        sum_kernel,
        out_shape=(jax.ShapeDtypeStruct(sums.shape, BF16), jax.ShapeDtypeStruct(sums.shape, F32)),
        in_specs=[VM] * 2,
        out_specs=(VM,) * 2,
        compiler_params=params(),
        cost_estimate=SMALL,
        name="sum_step",
    )(there, sums)


def result_kernel(length, there_ref, sums_ref, res_ref, ores_ref, odec_ref, oskip_ref):
    modes = res_ref.shape[0]
    sums = sums_ref[...] + there_ref[...].astype(F32)
    ores_ref[...] = sums[0:modes] * (1.0 / length)
    odec_ref[...] = sums[modes : 2 * modes] * (-1.0 / (length * length)) * res_ref[...]
    oskip_ref[...] = sums[2 * modes : 2 * modes + 1] * (1.0 / math.sqrt(length))


def results(there, sums, residues, length):
    modes, width = residues.shape
    return pl.pallas_call(
        functools.partial(result_kernel, length),
        out_shape=(
            jax.ShapeDtypeStruct((modes, width), F32),
            jax.ShapeDtypeStruct((modes, width), F32),
            jax.ShapeDtypeStruct((1, width), F32),
        ),
        in_specs=[VM] * 3,
        out_specs=(VM,) * 3,
        compiler_params=params(),
        cost_estimate=SMALL,
        name="results",
    )(there, sums, residues)


def prefix_step(me, there, state, carried, decays, tokens, length, hop, more):
    args = [there, state, *carried, decays]
    dtypes = (BF16, F32, F32) if more else (BF16, F32)
    return pl.pallas_call(
        functools.partial(prefix_kernel, length, tokens, hop, len(carried)),
        out_shape=tuple(jax.ShapeDtypeStruct(state.shape, dtype) for dtype in dtypes),
        in_specs=[SM] + [VM] * len(args),
        out_specs=(VM,) * len(dtypes),
        compiler_params=params(),
        cost_estimate=SMALL,
        name="prefix_step",
    )(me, *args)


def join_kernel(chunks, *refs):
    sent_ref, state_ref = refs[len(chunks) :]
    for part_ref, (low, high) in zip(refs, chunks):
        state_ref[:, low:high] = part_ref[...]
        sent_ref[:, low:high] = part_ref[...].astype(BF16)


def join_states(states, chunks):
    modes, width = states[0].shape[0], chunks[-1][1]
    return pl.pallas_call(
        functools.partial(join_kernel, chunks),
        out_shape=tuple(jax.ShapeDtypeStruct((modes, width), dtype) for dtype in (BF16, F32)),
        in_specs=[VM] * len(states),
        out_specs=(VM,) * 2,
        compiler_params=params(),
        cost_estimate=SMALL,
        name="join_states",
    )(*states)


def start_weights(blocks_ref, w_ref, w_buf, sems):
    width = w_buf.shape[1]
    copies = []
    for q in range(w_buf.shape[0]):
        start = pl.multiple_of(blocks_ref[q] * width, width)
        copies.append(pltpu.make_async_copy(w_ref.at[pl.ds(start, width)], w_buf.at[q], sems.at[q]))
        copies[-1].start()
    return copies


def finish_weights(copies, up_ref, w_buf, outs):
    width = w_buf.shape[-2]
    for copy in copies:
        copy.wait()
    rows = min(width, 256)
    for q, out in enumerate(outs):
        block = w_buf.at[q] if len(w_buf.shape) == 3 else w_buf
        for start in range(0, width, rows):
            out[:, start : start + rows] = lax.dot_general(
                up_ref[...], block[start : start + rows, :], (((1,), (1,)), ((), ())),
                preferred_element_type=F32,
            ).astype(out.dtype)


def fetch_kernel(block_ref, w_ref, o_ref, sem):
    width = o_ref.shape[0]
    start = pl.multiple_of(block_ref[0] * width, width)
    copy = pltpu.make_async_copy(w_ref.at[pl.ds(start, width)], o_ref, sem)
    copy.start()
    copy.wait()


def fetch(weight, width, block):
    return pl.pallas_call(
        fetch_kernel,
        out_shape=jax.ShapeDtypeStruct((width, weight.shape[1]), BF16),
        in_specs=[SM, pl.BlockSpec(memory_space=pl.ANY)],
        out_specs=VM,
        scratch_shapes=[pltpu.SemaphoreType.DMA],
        compiler_params=params(PROJECT_LIMIT),
        cost_estimate=takes(3),
        name="fetch",
    )(block, weight)


def project_kernel(pieces, blocks_ref, up_hbm, w_ref, *refs):
    outs, (w_buf, sems, up_ref, up_sem) = refs[:pieces], refs[pieces:]
    copy = pltpu.make_async_copy(up_hbm, up_ref, up_sem)
    copy.start()
    copies = start_weights(blocks_ref, w_ref, w_buf, sems)
    copy.wait()
    finish_weights(copies, up_ref, w_buf, outs)


def first_kernel(pieces, chunks, length, blocks_ref, held_ref, up_ref, w_ref, sig_ref, dec_ref, *refs):
    lents = pieces // 2 + 1
    lent_ref, *pairs = refs[:lents]
    end_ref, sent_ref, *tables = refs[lents:-4]
    w_buf, sems, ebuf, e1buf = refs[-4:]
    width = w_buf.shape[1]
    outs = [lent_ref.at[:, k * width : (k + 1) * width] for k in range(lents)] + pairs
    copies = start_weights(blocks_ref, w_ref, w_buf, sems)
    for k, (low, high) in enumerate(chunks):
        signal_chunk(length, low, high, sig_ref, dec_ref, end_ref, *tables[3 * k : 3 * k + 3], ebuf, e1buf)
    sent_ref[...] = end_ref[...].astype(BF16)
    finish_weights([], up_ref, held_ref, outs[:1])
    finish_weights(copies, up_ref, w_buf, outs[1:])


def weight_scratch(pieces, width, feats):
    return [pltpu.VMEM((pieces, width, feats), BF16), pltpu.SemaphoreType.DMA((pieces,))]


def project(up, weight, width, blocks):
    tokens, feats = up.shape
    pieces = blocks.shape[0]
    return pl.pallas_call(
        functools.partial(project_kernel, pieces),
        out_shape=[jax.ShapeDtypeStruct((tokens, width), BF16)] * pieces,
        in_specs=[SM] + [pl.BlockSpec(memory_space=pl.ANY)] * 2,
        out_specs=[VM] * pieces,
        scratch_shapes=weight_scratch(pieces, width, feats)
        + [pltpu.VMEM(up.shape, up.dtype), pltpu.SemaphoreType.DMA],
        compiler_params=params(PROJECT_LIMIT),
        cost_estimate=takes(4),
        name="project",
    )(blocks, up, weight)


def project_and_scan(up, weight, width, lead, rest, signal, decays, chunks, length):
    tokens, feats = up.shape
    modes = decays.shape[0]
    pieces = 1 + rest.shape[0]
    lents = pieces // 2 + 1
    shapes = [jax.ShapeDtypeStruct((tokens, lents * width), BF16)]
    shapes += [jax.ShapeDtypeStruct((tokens, width), BF16)] * (pieces - lents)
    shapes += [jax.ShapeDtypeStruct((2 * modes, width), dtype) for dtype in (F32, BF16)]
    for low, high in chunks:
        states = jax.ShapeDtypeStruct((modes * SUB, high - low), BF16)
        shapes += [jax.ShapeDtypeStruct((tokens, high - low), BF16), states, states]
    out = pl.pallas_call(
        functools.partial(first_kernel, pieces, chunks, length),
        out_shape=shapes,
        in_specs=[SM, VM, VM, pl.BlockSpec(memory_space=pl.ANY), VM, VM],
        out_specs=[VM] * len(shapes),
        scratch_shapes=weight_scratch(pieces - 1, width, feats)
        + [pltpu.VMEM((modes * SUB, LANES), F32)] * 2,
        compiler_params=params(PROJECT_LIMIT),
        cost_estimate=takes(8),
        name="project_and_scan",
    )(rest, fetch(weight, width, lead), up, weight, signal, decays)
    start = 1 + pieces - lents
    tables = out[start + 2 :]
    return out[0], out[1:start], out[start : start + 2], [
        tables[3 * k : 3 * k + 3] for k in range(len(chunks))
    ]


def pair_kernel(chunks, lent, mine_ref, lent_ref, *outs):
    base = mine_ref.shape[1] * lent
    for (low, high), out in zip(chunks, outs):
        total = mine_ref[:, low:high].astype(F32) + lent_ref[:, base + low : base + high].astype(F32)
        out[...] = total.astype(BF16)


def pair_sums(mine, lent, index, chunks):
    tokens = mine.shape[0]
    return pl.pallas_call(
        functools.partial(pair_kernel, chunks, index),
        out_shape=[jax.ShapeDtypeStruct((tokens, high - low), BF16) for low, high in chunks],
        in_specs=[VM] * 2,
        out_specs=[VM] * len(chunks),
        compiler_params=params(),
        cost_estimate=SMALL,
        name="pair_sums",
    )(mine, lent)


def send(x, axis, size, hop):
    return lax.ppermute(x, axis, [(i, i ^ hop) for i in range(size)])


def cuts(width):
    lane_blocks = width // LANES
    first = lane_blocks // 2 * LANES
    return [(0, first), (first, width)]


def body(signal, upstream, out_weight, residues, decays, skip_gain):
    tokens, width = signal.shape
    groups = lax.axis_size("ctx")
    blocks = lax.axis_size("ch")
    length = tokens * groups
    modes = residues.shape[1]
    me = lax.axis_index("ch")
    place = jnp.reshape(lax.axis_index("ctx").astype(jnp.int32), (1,))
    dec = decays.T
    res = residues.T
    gain = skip_gain[None, :]
    chunks = cuts(width)
    hops = range(2, blocks, 2)
    levels = [1 << k for k in range(groups.bit_length() - 1)]

    wanted = [me ^ hop ^ 1 for hop in hops] + [me ^ 1] + [me ^ hop for hop in hops]
    rest = jnp.stack(wanted[1:]).astype(jnp.int32)
    lead, mine = [jnp.reshape(b, (1,)).astype(jnp.int32) for b in (wanted[0], me)]
    lead, rest, mine, place = lax.optimization_barrier((lead, rest, mine, place))
    lent, parts, (state, sent), tables = project_and_scan(
        upstream, out_weight, width, lead, rest, signal, dec, chunks, length
    )
    lent = send(lent, "ch", blocks, 1)
    pairs = [pair_sums(part, lent, index, chunks) for index, part in enumerate(parts)]
    upstream, pairs = lax.optimization_barrier((upstream, pairs))
    arrived = [[send(pair[k], "ch", blocks, hop) for pair, hop in zip(pairs, hops)] for k in range(len(chunks))]
    (own,) = project(upstream, out_weight, width, mine)

    before, pays, states, locs = [], [], [], []

    def take(chunk, low, high, sigp, y, y1):
        grad, z, own_state = gradient_states([own, lent, *chunk], len(hops), high - low, low, dec, length)
        states.append(own_state)
        pays.append(filter_sums(grad, sigp, dec, y, y1, length, low))
        locs.append((grad, z, low))

    for hop in levels:
        if hop == levels[-1]:
            sent, own = lax.optimization_barrier((sent, own))
            pass
        there = send(sent, "ctx", groups, hop)
        if hop == 1:
            there, pairs = lax.optimization_barrier((there, pairs))
        if hop != levels[-1]:
            sent, after, *rest = prefix_step(
                place, there, state, before, dec, tokens, length, hop, hop * 2 != levels[-1]
            )
            state, before = (rest + [None])[0], [after]
    ends = there
    for k in range(len(pays), len(chunks)):
        pays, arrived[k] = lax.optimization_barrier((pays, arrived[k]))
        take(arrived[k], *chunks[k], *tables[k])
    sent, state = join_states(states, chunks)
    locs = [local_part(grad, z, dec, res, gain, length, low) for grad, z, low in locs]
    there = send(sent, "ctx", groups, levels[0])
    sent, state, later, sums = merge(
        place, there, state, ends, pays, dec, before, chunks, tokens, length, levels[0], levels[-1]
    )
    for hop in levels[1:]:
        there = send(sent, "ctx", groups, hop)
        if hop != levels[-1]:
            sent, later, sums, *state = tail_step(
                place, there, state, later, sums, dec, tokens, length, hop, hop * 2 != levels[-1]
            )
            state = state[0] if state else None
    moved, sums = sum_step(there, sums)
    out = finish(place, there, later, dec, res, locs, chunks, tokens, length, levels[-1])
    ores, odec, oskip = results(send(moved, "ctx", groups, levels[0]), sums, res, length)
    return (out, ores.T, odec.T, oskip[0])


def solution(mesh):
    placed = (P("ctx", "ch"), P("ctx", "ch"), P(None, "ch"), P("ch", None), P("ch", None), P("ch"))
    return jax.shard_map(
        body,
        mesh=mesh,
        in_specs=placed,
        out_specs=(P("ctx", "ch"), P("ch", None), P("ch", None), P("ch")),
        check_vma=False,
    )
```

```python
import functools
import math

import jax
import jax.numpy as jnp
from jax import lax
from jax.experimental import pallas as pl
from jax.experimental.pallas import tpu as pltpu
from jax.sharding import PartitionSpec as P

F32 = jnp.float32
BF16 = jnp.bfloat16
SUB = 16
HALF = 8
LANES = 128
VMEM_LIMIT = 12 * 1024 * 1024
PROJECT_LIMIT = 43 * 1024 * 1024
VM = pl.BlockSpec(memory_space=pltpu.VMEM)
SM = pl.BlockSpec(memory_space=pltpu.SMEM)
HBM = pl.BlockSpec(memory_space=pl.ANY)


def interleave(tokens, transpose=False):
    steps = tokens // SUB
    row = lax.broadcasted_iota(jnp.int32, (tokens, tokens), 1 if transpose else 0)
    col = lax.broadcasted_iota(jnp.int32, (tokens, tokens), 0 if transpose else 1)
    source = (row & (SUB - 1)) * steps + lax.shift_right_logical(row, SUB.bit_length() - 1)
    return jnp.where(col == source, 1.0, 0.0).astype(BF16)


def group_sums(groups, size):
    col = lax.broadcasted_iota(jnp.int32, (groups, groups * size), 1)
    row = lax.broadcasted_iota(jnp.int32, (groups, groups * size), 0)
    return jnp.where(lax.shift_right_logical(col, size.bit_length() - 1) == row, 1.0, 0.0).astype(F32)


def params(limit=VMEM_LIMIT):
    return pltpu.CompilerParams(vmem_limit_bytes=limit)


SMALL = pl.CostEstimate(flops=1, bytes_accessed=1, transcendentals=0)


def takes(microseconds):
    return pl.CostEstimate(flops=int(microseconds * 1e9), bytes_accessed=1, transcendentals=0)


def spread(row):
    return jnp.broadcast_to(row, (HALF, row.shape[-1]))


def pairwise(terms):
    while len(terms) > 1:
        rest = terms[len(terms) // 2 * 2 :]
        terms = [a + b for a, b in zip(terms[::2], terms[1::2])] + rest
    return terms[0]


def lane_block(block):
    return pl.ds(pl.multiple_of(block * LANES, LANES), LANES)


def rows_of(i, half):
    return pl.ds(SUB * i + HALF * half, HALF)


def recur(poles, values):
    last = values[-1]
    sums = [last] * len(poles)
    firsts = None
    for value in values[-2::-1]:
        if firsts is None:
            moved = [p * s for p, s in zip(poles, sums)]
            firsts = moved
        else:
            firsts = [p * (f + s) for p, f, s in zip(poles, firsts, sums)]
            moved = [p * s for p, s in zip(poles, sums)]
        sums = [m + value for m in moved]
    return sums, firsts


def signal_chunk(length, low, high, sig_ref, dec_ref, end_ref, sigp_ref, y_ref, y1_ref, ebuf, e1buf):
    tokens, width = sig_ref.shape[0], high - low
    modes = dec_ref.shape[0]
    steps = tokens // SUB
    sigp_ref[...] = jnp.dot(
        interleave(tokens), sig_ref[:, low:high], preferred_element_type=F32
    ).astype(BF16)

    @pl.loop(0, width // LANES)
    def _(block):
        lanes = lane_block(block)
        there = lane_block(block + low // LANES)
        rate = dec_ref[:, there] * (1.0 / length)
        pole_all = jnp.exp(-rate)
        pole_sub = jnp.exp(-rate * steps)
        both = [sigp_ref[pl.ds(SUB * i, SUB), lanes].astype(F32) for i in range(steps)]
        for half in range(2):
            values = [both[i][HALF * half : HALF * (half + 1)] for i in reversed(range(steps))]
            for first in range(0, modes, 8):
                poles = [spread(pole_all[n : n + 1]) for n in range(first, first + 8)]
                sums, firsts = recur(poles, values)
                for n in range(8):
                    rows = rows_of(first + n, half)
                    end = poles[n] * sums[n]
                    ebuf[rows, :] = end
                    e1buf[rows, :] = poles[n] * firsts[n] + end
        carry = jnp.zeros((modes, LANES), F32)
        carry1 = jnp.zeros((modes, LANES), F32)
        for j in range(SUB):
            pick = pl.ds(j, modes, stride=SUB)
            end, end1 = ebuf[pick, :], e1buf[pick, :]
            ebuf[pick, :] = carry
            e1buf[pick, :] = carry1
            carry1 = pole_sub * (carry1 + steps * carry) + end1
            carry = pole_sub * carry + end
        y_ref[:, lanes] = ebuf[...].astype(BF16)
        y1_ref[:, lanes] = e1buf[...].astype(BF16)
        end_ref[0:modes, there] = carry
        end_ref[modes : 2 * modes, there] = carry1


def gradient_kernel(length, base, parts, *refs):
    own_ref, lent_ref, *got_refs = refs[: 1 + parts]
    dec_ref, grad_ref, z_ref, state_ref, sbuf = refs[1 + parts :]
    tokens, width = grad_ref.shape
    modes = dec_ref.shape[0]
    steps = tokens // SUB
    place = lax.broadcasted_iota(jnp.int32, (HALF, LANES), 0).astype(F32) * steps
    total = own_ref[:, base : base + width].astype(F32)
    total = total + lent_ref[:, base : base + width].astype(F32)
    for got in got_refs:
        total = total + got[...].astype(F32)
    grad_ref[...] = jnp.dot(
        interleave(tokens), total.astype(BF16), preferred_element_type=F32
    )

    @pl.loop(0, width // LANES)
    def _(block):
        here = lane_block(block)
        rate = dec_ref[:, lane_block(block + base // LANES)] * (-1.0 / length)
        pole_all = jnp.exp(rate)
        for half in range(2):
            values = [grad_ref[rows_of(i, half), here] for i in range(steps)]
            for first in range(0, modes, 8):
                poles = [spread(pole_all[n : n + 1]) for n in range(first, first + 8)]
                sums = [values[-1]] * 8
                for value in values[-2::-1]:
                    sums = [p * v + value for p, v in zip(poles, sums)]
                for n in range(8):
                    out = pl.ds(HALF * (first + n), HALF)
                    reach = jnp.exp(spread(rate[first + n : first + n + 1]) * (place + half * HALF * steps))
                    moved = reach * sums[n]
                    z_ref[block, rows_of(first + n, half), :] = moved
                    sbuf[out, here] = moved if half == 0 else sbuf[out, here] + moved

    state_ref[...] = jnp.dot(group_sums(modes, HALF), sbuf[...], preferred_element_type=F32)


def gradient_states(pieces, width, base, decays, length):
    tokens = pieces[0].shape[0]
    modes = decays.shape[0]
    return pl.pallas_call(
        functools.partial(gradient_kernel, length, base, len(pieces) - 1),
        out_shape=(
            jax.ShapeDtypeStruct((tokens, width), F32),
            jax.ShapeDtypeStruct((width // LANES, modes * SUB, LANES), F32),
            jax.ShapeDtypeStruct((modes, width), F32),
        ),
        in_specs=[VM] * (len(pieces) + 1),
        out_specs=(VM,) * 3,
        scratch_shapes=[pltpu.VMEM((modes * HALF, width), F32)],
        compiler_params=params(),
        cost_estimate=takes(1),
        name="gradient_states",
    )(*pieces, decays)


def filter_kernel(length, base, grad_ref, sigp_ref, dec_ref, y_ref, y1_ref, pay_ref, s1buf, rbuf, dbuf, gf):
    tokens, width = grad_ref.shape
    modes = dec_ref.shape[0]
    steps = tokens // SUB
    place = lax.broadcasted_iota(jnp.int32, (HALF, LANES), 0).astype(F32) * steps

    @pl.loop(0, width // LANES)
    def _(block):
        here = lane_block(block)
        rate = dec_ref[:, lane_block(block + base // LANES)] * (-1.0 / length)
        pole_all = jnp.exp(rate)
        both = [sigp_ref[pl.ds(SUB * i, SUB), here].astype(F32) for i in range(steps)]
        for half in range(2):
            values = [grad_ref[rows_of(i, half), here] for i in range(steps)]
            for first in range(0, modes, 8):
                poles = [spread(pole_all[n : n + 1]) for n in range(first, first + 8)]
                sums, firsts = recur(poles, values)
                for n in range(8):
                    rows = rows_of(first + n, half)
                    out = pl.ds(HALF * (first + n), HALF)
                    before, before1 = y_ref[rows, here].astype(F32), y1_ref[rows, here].astype(F32)
                    ahead = place + half * HALF * steps
                    reach = jnp.exp(spread(rate[first + n : first + n + 1]) * ahead)
                    terms = (
                        (s1buf, reach * (firsts[n] + ahead * sums[n])),
                        (rbuf, sums[n] * before),
                        (dbuf, sums[n] * before1 + firsts[n] * before),
                    )
                    for ref, term in terms:
                        ref[out, here] = term if half == 0 else ref[out, here] + term
            seen = [v[HALF * half : HALF * (half + 1)] for v in both]
            for lag in range(steps):
                term = pairwise([values[i + lag] * seen[i] for i in range(steps - lag)])
                out = pl.ds(HALF * lag, HALF)
                gf[out, here] = term if half == 0 else gf[out, here] + term

    adder = group_sums(modes, HALF)
    add = lambda m, ref: jnp.dot(m, ref[...], preferred_element_type=F32)
    lags = add(group_sums(steps, HALF), gf)
    res, dec, first = add(adder, rbuf), add(adder, dbuf), add(adder, s1buf)
    pole = jnp.exp(dec_ref[:, base : base + width] * (-1.0 / length))
    res = res + lags[0:1]
    weight = pole
    for lag in range(1, steps):
        term = weight * lags[lag : lag + 1]
        res = res + term
        dec = dec + lag * term
        weight = weight * pole
    for k, rows in enumerate((res, dec, first)):
        pay_ref[k * modes : (k + 1) * modes, :] = rows
    pay_ref[3 * modes :, :] = jnp.broadcast_to(lags[0:1], (8, width))


def filter_sums(grad, sigp, decays, y, y1, length, base):
    tokens, width = grad.shape
    modes = decays.shape[0]
    buf = pltpu.VMEM((modes * HALF, width), F32)
    return pl.pallas_call(
        functools.partial(filter_kernel, length, base),
        out_shape=jax.ShapeDtypeStruct((3 * modes + 8, width), F32),
        in_specs=[VM] * 5,
        out_specs=VM,
        scratch_shapes=[buf] * 3 + [pltpu.VMEM((tokens // SUB * HALF, width), F32)],
        compiler_params=params(),
        cost_estimate=takes(3),
        name="filter_sums",
    )(grad, sigp, decays, y, y1)


def carry_out(outs, poles, starts):
    outs = list(outs)
    for i in reversed(range(len(outs))):
        outs[i] = outs[i] + pairwise(starts)
        if i:
            starts = [p * s for p, s in zip(poles, starts)]
    return outs


def local_kernel(length, base, grad_ref, z_ref, dec_ref, res_ref, gain_ref, loc_ref, cbuf):
    tokens, width = grad_ref.shape
    modes = dec_ref.shape[0]
    steps = tokens // SUB

    @pl.loop(0, width // LANES)
    def _(block):
        here = lane_block(block)
        lanes = lane_block(block + base // LANES)
        rate = dec_ref[:, lanes] * (1.0 / length)
        pole_all = jnp.exp(-rate)
        weight = res_ref[:, lanes] * (1.0 / math.sqrt(length))
        gain = spread(gain_ref[:, lanes])
        sums = jnp.zeros((modes, LANES), F32)
        for j in reversed(range(SUB)):
            pick = pl.ds(j, modes, stride=SUB)
            back = jnp.exp(rate * (steps * (j + 1) - 1))
            cbuf[pick, :] = weight * (back * sums)
            sums = sums + z_ref[block, pick, :]
        filt = []
        for _ in range(steps):
            filt.append(spread(jnp.sum(weight, axis=0, keepdims=True)))
            weight = weight * pole_all
        for half in range(2):
            values = [grad_ref[rows_of(i, half), here] for i in range(steps)]
            outs = [
                pairwise([filt[lag] * values[i + lag] for lag in range(steps - i)]) for i in range(steps)
            ]
            for first in range(0, modes, 8):
                picked = range(first, first + 8)
                poles = [spread(pole_all[n : n + 1]) for n in picked]
                outs = carry_out(outs, poles, [cbuf[rows_of(n, half), :] for n in picked])
            for i in range(steps):
                loc_ref[rows_of(i, half), here] = outs[i] + gain * values[i]


def local_part(grad, z, decays, residues, gain, length, base):
    tokens, width = grad.shape
    modes = decays.shape[0]
    return pl.pallas_call(
        functools.partial(local_kernel, length, base),
        out_shape=jax.ShapeDtypeStruct((tokens, width), F32),
        in_specs=[VM] * 5,
        out_specs=VM,
        scratch_shapes=[pltpu.VMEM((modes * SUB, LANES), F32)],
        compiler_params=params(),
        cost_estimate=takes(1.5),
        name="local_part",
    )(grad, z, decays, residues, gain)


def finish_kernel(length, hop, chunks, me_ref, there_ref, later_ref, dec_ref, res_ref, *refs):
    locs = refs[: len(chunks)]
    o_ref, vals = refs[len(chunks) :]
    tokens = o_ref.shape[0]
    modes = dec_ref.shape[0]
    steps = tokens // SUB
    scale = 1.0 / math.sqrt(length)
    ahead = (SUB - 1 - lax.broadcasted_iota(jnp.int32, (HALF, LANES), 0)).astype(F32) * steps
    vals[...] = later_step(
        me_ref, there_ref.at[0:modes, :], later_ref[...], dec_ref, length, tokens, hop
    )

    for loc_ref, (low, high) in zip(locs, chunks):
        @pl.loop(0, (high - low) // LANES)
        def _(block):
            here = lane_block(block)
            lanes = lane_block(block + low // LANES)
            rate = dec_ref[:, lanes] * (-1.0 / length)
            pole_all = jnp.exp(rate)
            lead = scale * res_ref[:, lanes] * pole_all * vals[:, lanes]
            for half in range(2):
                outs = [loc_ref[rows_of(i, half), here] for i in range(steps)]
                for first in range(0, modes, 8):
                    picked = range(first, first + 8)
                    poles = [spread(pole_all[n : n + 1]) for n in picked]
                    starts = [
                        spread(lead[n : n + 1]) * jnp.exp(spread(rate[n : n + 1]) * (ahead - half * HALF * steps))
                        for n in picked
                    ]
                    outs = carry_out(outs, poles, starts)
                for i in range(steps):
                    loc_ref[rows_of(i, half), here] = outs[i]

    turn = interleave(tokens, transpose=True)
    for loc_ref, (low, high) in zip(locs, chunks):
        o_ref[:, low:high] = jnp.dot(
            turn, loc_ref[...].astype(BF16), preferred_element_type=F32
        ).astype(BF16)


def finish(me, there, later, decays, residues, locs, chunks, tokens, length, hop):
    modes, width = decays.shape
    return pl.pallas_call(
        functools.partial(finish_kernel, length, hop, chunks),
        out_shape=jax.ShapeDtypeStruct((tokens, width), BF16),
        in_specs=[SM] + [VM] * (4 + len(locs)),
        out_specs=VM,
        scratch_shapes=[pltpu.VMEM((modes, width), F32)],
        compiler_params=params(),
        cost_estimate=takes(3),
        name="finish",
    )(me, there, later, decays, residues, *locs)


def place_bits(me_ref, hop):
    me = me_ref[0]
    return (me & (hop - 1)).astype(F32), (me & hop) != 0


def before_step(me_ref, there_ref, before_refs, dec_ref, length, tokens, hop):
    modes = dec_ref.shape[0]
    inside, upper = place_bits(me_ref, hop)
    reach = jnp.exp(dec_ref[...] * (-1.0 / length) * (inside * tokens))
    other, other1 = there_ref[0:modes, :].astype(F32), there_ref[modes : 2 * modes, :].astype(F32)
    before = jnp.where(upper, reach * other, 0.0)
    before1 = jnp.where(upper, reach * (other1 + (inside * tokens) * other), 0.0)
    for ref in before_refs:
        before = before + ref[0:modes, :]
        before1 = before1 + ref[modes : 2 * modes, :]
    return before, before1


def prefix_kernel(length, tokens, hop, carried, me_ref, there_ref, state_ref, *refs):
    refs, (sent_ref, after_ref, *next_ref) = refs[: 1 + carried], refs[1 + carried :]
    *before_refs, dec_ref = refs
    modes = dec_ref.shape[0]
    rows, rows1 = slice(0, modes), slice(modes, 2 * modes)
    after_ref[rows, :], after_ref[rows1, :] = before_step(
        me_ref, there_ref, before_refs, dec_ref, length, tokens, hop
    )
    other, other1 = there_ref[rows, :].astype(F32), there_ref[rows1, :].astype(F32)
    state, first = state_ref[rows, :], state_ref[rows1, :]
    _, upper = place_bits(me_ref, hop)
    span = jnp.exp(dec_ref[...] * (-1.0 / length) * (hop * tokens))
    late, early = jnp.where(upper, state, other), jnp.where(upper, other, state)
    late1, early1 = jnp.where(upper, first, other1), jnp.where(upper, other1, first)
    first = late1 + span * (early1 + (hop * tokens) * early)
    state = late + span * early
    for part, value in ((rows, state), (rows1, first)):
        for ref in next_ref:
            ref[part, :] = value
        sent_ref[part, :] = value.astype(BF16)


def later_step(me_ref, there_ref, later, dec_ref, length, tokens, hop):
    inside, upper = place_bits(me_ref, hop)
    reach = jnp.exp(dec_ref[...] * (-1.0 / length) * ((hop - 1 - inside) * tokens))
    return later + jnp.where(upper, 0.0, reach * there_ref[...].astype(F32))


def suffix_step(me_ref, other, state, dec_ref, length, tokens, hop):
    _, upper = place_bits(me_ref, hop)
    span = jnp.exp(dec_ref[...] * (-1.0 / length) * (hop * tokens))
    return jnp.where(upper, other, state) + span * jnp.where(upper, state, other)


def merge_kernel(
    length, tokens, hop, last, chunks, me_ref, there_ref, state_ref, ends_ref, *refs
):
    sent_ref, next_ref, later_ref, sums_ref = refs[-4:]
    pays, (dec_ref, *before_refs) = refs[: len(chunks)], refs[len(chunks) : -4]
    modes = dec_ref.shape[0]
    all_before, all_before1 = before_step(me_ref, ends_ref, before_refs, dec_ref, length, tokens, last)
    nothing = jnp.zeros_like(later_ref)
    later_ref[...] = later_step(me_ref, there_ref, nothing, dec_ref, length, tokens, hop)
    state = suffix_step(
        me_ref, there_ref[...].astype(F32), state_ref[...], dec_ref, length, tokens, hop
    )
    next_ref[...] = state
    sent_ref[0:modes, :] = state.astype(BF16)
    for pay_ref, (low, high) in zip(pays, chunks):
        res, dec, first = [pay_ref[k * modes : (k + 1) * modes, :] for k in range(3)]
        skip = pay_ref[3 * modes :, :]
        before, before1 = all_before[:, low:high], all_before1[:, low:high]
        start = state_ref[:, low:high]
        res = res + start * before
        dec = dec + first * before + start * before1
        for at, value in ((0, res), (modes, dec), (2 * modes, skip)):
            end = at + value.shape[0]
            sums_ref[at:end, low:high] = value
            sent_ref[modes + at : modes + end, low:high] = value.astype(BF16)


def merge(me, there, state, ends, pays, decays, before, chunks, tokens, length, hop, last):
    modes, width = decays.shape
    args = (there, state, ends, *pays, decays, *before)
    return pl.pallas_call(
        functools.partial(merge_kernel, length, tokens, hop, last, chunks),
        out_shape=tuple(
            jax.ShapeDtypeStruct((rows, width), dtype)
            for rows, dtype in ((3 * modes + 8, BF16), (modes, F32), (modes, F32), (2 * modes + 8, F32))
        ),
        in_specs=[SM] + [VM] * len(args),
        out_specs=(VM,) * 4,
        compiler_params=params(),
        cost_estimate=SMALL,
        name="merge",
    )(me, *args)


def tail_kernel(
    length, tokens, hop, me_ref, there_ref, state_ref, later_ref, sums_ref, dec_ref,
    sent_ref, after_ref, total_ref, *next_ref,
):
    modes = dec_ref.shape[0]
    there = there_ref.at[0:modes, :]
    after_ref[...] = later_step(me_ref, there, later_ref[...], dec_ref, length, tokens, hop)
    state = suffix_step(me_ref, there[...].astype(F32), state_ref[...], dec_ref, length, tokens, hop)
    if next_ref:
        next_ref[0][...] = state
    sent_ref[0:modes, :] = state.astype(BF16)
    sums = sums_ref[...] + there_ref[modes:, :].astype(F32)
    total_ref[...] = sums
    sent_ref[modes:, :] = sums.astype(BF16)


def tail_step(me, there, state, later, sums, decays, tokens, length, hop, more):
    args = (there, state, later, sums, decays)
    outs = (there, later, sums) + ((state,) if more else ())
    return pl.pallas_call(
        functools.partial(tail_kernel, length, tokens, hop),
        out_shape=tuple(jax.ShapeDtypeStruct(x.shape, x.dtype) for x in outs),
        in_specs=[SM] + [VM] * 5,
        out_specs=(VM,) * len(outs),
        compiler_params=params(),
        cost_estimate=SMALL,
        name="tail_step",
    )(me, *args)


def sum_kernel(there_ref, sums_ref, sent_ref, total_ref):
    sums = sums_ref[...] + there_ref[there_ref.shape[0] - sums_ref.shape[0] :, :].astype(F32)
    total_ref[...] = sums
    sent_ref[...] = sums.astype(BF16)


def sum_step(there, sums):
    return pl.pallas_call(
        sum_kernel,
        out_shape=(jax.ShapeDtypeStruct(sums.shape, BF16), jax.ShapeDtypeStruct(sums.shape, F32)),
        in_specs=[VM] * 2,
        out_specs=(VM,) * 2,
        compiler_params=params(),
        cost_estimate=SMALL,
        name="sum_step",
    )(there, sums)


def result_kernel(length, there_ref, sums_ref, res_ref, ores_ref, odec_ref, oskip_ref):
    modes = res_ref.shape[0]
    sums = sums_ref[...] + there_ref[...].astype(F32)
    ores_ref[...] = sums[0:modes] * (1.0 / length)
    odec_ref[...] = sums[modes : 2 * modes] * (-1.0 / (length * length)) * res_ref[...]
    oskip_ref[...] = sums[2 * modes : 2 * modes + 1] * (1.0 / math.sqrt(length))


def results(there, sums, residues, length):
    modes, width = residues.shape
    return pl.pallas_call(
        functools.partial(result_kernel, length),
        out_shape=(
            jax.ShapeDtypeStruct((modes, width), F32),
            jax.ShapeDtypeStruct((modes, width), F32),
            jax.ShapeDtypeStruct((1, width), F32),
        ),
        in_specs=[VM] * 3,
        out_specs=(VM,) * 3,
        compiler_params=params(),
        cost_estimate=SMALL,
        name="results",
    )(there, sums, residues)


def prefix_step(me, there, state, carried, decays, tokens, length, hop, more):
    args = [there, state, *carried, decays]
    dtypes = (BF16, F32, F32) if more else (BF16, F32)
    return pl.pallas_call(
        functools.partial(prefix_kernel, length, tokens, hop, len(carried)),
        out_shape=tuple(jax.ShapeDtypeStruct(state.shape, dtype) for dtype in dtypes),
        in_specs=[SM] + [VM] * len(args),
        out_specs=(VM,) * len(dtypes),
        compiler_params=params(),
        cost_estimate=SMALL,
        name="prefix_step",
    )(me, *args)


def join_kernel(chunks, *refs):
    sent_ref, state_ref = refs[len(chunks) :]
    for part_ref, (low, high) in zip(refs, chunks):
        state_ref[:, low:high] = part_ref[...]
        sent_ref[:, low:high] = part_ref[...].astype(BF16)


def join_states(states, chunks):
    modes, width = states[0].shape[0], chunks[-1][1]
    return pl.pallas_call(
        functools.partial(join_kernel, chunks),
        out_shape=tuple(jax.ShapeDtypeStruct((modes, width), dtype) for dtype in (BF16, F32)),
        in_specs=[VM] * len(states),
        out_specs=(VM,) * 2,
        compiler_params=params(),
        cost_estimate=SMALL,
        name="join_states",
    )(*states)


def weight_copies(blocks_ref, w_ref, width, targets, sems):
    copies = []
    for q, target in enumerate(targets):
        start = pl.multiple_of(blocks_ref[q] * width, width)
        copies.append(pltpu.make_async_copy(w_ref.at[pl.ds(start, width)], target, sems.at[q]))
    return copies


def project_block(up_ref, w_rows, out_ref):
    width = w_rows.shape[0]
    rows = min(width, 256)
    for start in range(0, width, rows):
        out_ref[:, start : start + rows] = lax.dot_general(
            up_ref[...], w_rows[start : start + rows, :], (((1,), (1,)), ((), ())),
            preferred_element_type=F32,
        ).astype(out_ref.dtype)


def fetch_kernel(blocks_ref, w_ref, o_ref, sems):
    pieces = blocks_ref.shape[0]
    width = o_ref.shape[0] // pieces
    targets = [o_ref.at[q * width : (q + 1) * width, :] for q in range(pieces)]
    copies = weight_copies(blocks_ref, w_ref, width, targets, sems)
    for copy in copies:
        copy.start()
    for copy in copies:
        copy.wait()


def fetch(weight, width, blocks):
    pieces = blocks.shape[0]
    return pl.pallas_call(
        fetch_kernel,
        out_shape=jax.ShapeDtypeStruct((pieces * width, weight.shape[1]), BF16),
        in_specs=[SM, HBM],
        out_specs=VM,
        scratch_shapes=[pltpu.SemaphoreType.DMA((pieces,))],
        compiler_params=params(PROJECT_LIMIT),
        cost_estimate=takes(3),
        name="fetch",
    )(blocks, weight)


def multiply_kernel(up_ref, held_ref, o_ref):
    project_block(up_ref, held_ref, o_ref)


def multiply(up, held):
    return pl.pallas_call(
        multiply_kernel,
        out_shape=jax.ShapeDtypeStruct((up.shape[0], held.shape[0]), BF16),
        in_specs=[VM] * 2,
        out_specs=VM,
        compiler_params=params(),
        cost_estimate=takes(1),
        name="multiply",
    )(up, held)


def scan_kernel(pieces, chunks, length, blocks_ref, up_ref, w_ref, sig_ref, dec_ref, *refs):
    outs, (end_ref, sent_ref, *tables) = refs[:pieces], refs[pieces:-4]
    w_buf, sems, ebuf, e1buf = refs[-4:]
    width = w_buf.shape[1]
    copies = weight_copies(blocks_ref, w_ref, width, [w_buf.at[q] for q in range(pieces)], sems)
    for copy in copies:
        copy.start()
    for k, (low, high) in enumerate(chunks):
        signal_chunk(length, low, high, sig_ref, dec_ref, end_ref, *tables[3 * k : 3 * k + 3], ebuf, e1buf)
    sent_ref[...] = end_ref[...].astype(BF16)
    for copy in copies:
        copy.wait()
    for q, out in enumerate(outs):
        project_block(up_ref, w_buf.at[q], out)


def project_and_scan(up, weight, width, blocks, signal, decays, chunks, length):
    tokens, feats = up.shape
    modes = decays.shape[0]
    pieces = blocks.shape[0]
    shapes = [jax.ShapeDtypeStruct((tokens, width), BF16)] * pieces
    shapes += [jax.ShapeDtypeStruct((2 * modes, width), dtype) for dtype in (F32, BF16)]
    for low, high in chunks:
        states = jax.ShapeDtypeStruct((modes * SUB, high - low), BF16)
        shapes += [jax.ShapeDtypeStruct((tokens, high - low), BF16), states, states]
    out = pl.pallas_call(
        functools.partial(scan_kernel, pieces, chunks, length),
        out_shape=shapes,
        in_specs=[SM, VM, HBM, VM, VM],
        out_specs=[VM] * len(shapes),
        scratch_shapes=[
            pltpu.VMEM((pieces, width, feats), BF16),
            pltpu.SemaphoreType.DMA((pieces,)),
        ]
        + [pltpu.VMEM((modes * SUB, LANES), F32)] * 2,
        compiler_params=params(PROJECT_LIMIT),
        cost_estimate=takes(6),
        name="project_and_scan",
    )(blocks, up, weight, signal, decays)
    tables = out[pieces + 2 :]
    return out[:pieces], out[pieces : pieces + 2], [
        tables[3 * k : 3 * k + 3] for k in range(len(chunks))
    ]


def last_kernel(block_ref, up_ref, w_ref, o_ref, w_buf, sems):
    (copy,) = weight_copies(block_ref, w_ref, w_buf.shape[0], [w_buf], sems)
    copy.start()
    copy.wait()
    project_block(up_ref, w_buf, o_ref)


def project_last(up, weight, width, block):
    tokens, feats = up.shape
    return pl.pallas_call(
        last_kernel,
        out_shape=jax.ShapeDtypeStruct((tokens, width), BF16),
        in_specs=[SM, VM, HBM],
        out_specs=VM,
        scratch_shapes=[pltpu.VMEM((width, feats), BF16), pltpu.SemaphoreType.DMA((1,))],
        compiler_params=params(PROJECT_LIMIT),
        cost_estimate=takes(4),
        name="project_last",
    )(block, up, weight)


def pair_kernel(chunks, lent, mine_ref, lent_ref, *outs):
    base = mine_ref.shape[1] * lent
    for (low, high), out in zip(chunks, outs):
        total = mine_ref[:, low:high].astype(F32) + lent_ref[:, base + low : base + high].astype(F32)
        out[...] = total.astype(BF16)


def pair_sums(mine, lent, index, chunks):
    tokens = mine.shape[0]
    return pl.pallas_call(
        functools.partial(pair_kernel, chunks, index),
        out_shape=[jax.ShapeDtypeStruct((tokens, high - low), BF16) for low, high in chunks],
        in_specs=[VM] * 2,
        out_specs=[VM] * len(chunks),
        compiler_params=params(),
        cost_estimate=SMALL,
        name="pair_sums",
    )(mine, lent)


def send(x, axis, size, hop):
    return lax.ppermute(x, axis, [(i, i ^ hop) for i in range(size)])


def cuts(width):
    lane_blocks = width // LANES
    first = lane_blocks // 2 * LANES
    return [(0, first), (first, width)]


def body(signal, upstream, out_weight, residues, decays, skip_gain):
    tokens, width = signal.shape
    groups = lax.axis_size("ctx")
    blocks = lax.axis_size("ch")
    length = tokens * groups
    modes = residues.shape[1]
    me = lax.axis_index("ch")
    place = jnp.reshape(lax.axis_index("ctx").astype(jnp.int32), (1,))
    dec = decays.T
    res = residues.T
    gain = skip_gain[None, :]
    chunks = cuts(width)
    hops = range(2, blocks, 2)
    levels = [1 << k for k in range(groups.bit_length() - 1)]

    index = lambda blocks: jnp.stack(blocks).astype(jnp.int32)
    first, second, third = index([me ^ hop ^ 1 for hop in hops]), index([me ^ hop for hop in hops] + [me ^ 1]), index([me])
    first, second, third, place = lax.optimization_barrier((first, second, third, place))
    lent = send(multiply(upstream, fetch(out_weight, width, first)), "ch", blocks, 1)
    (*parts, mine), (state, sent), tables = project_and_scan(
        upstream, out_weight, width, second, signal, dec, chunks, length
    )
    pairs = [pair_sums(part, lent, index, chunks) for index, part in enumerate(parts)]
    upstream, pairs = lax.optimization_barrier((upstream, pairs))
    arrived = [[send(pair[k], "ch", blocks, hop) for pair, hop in zip(pairs, hops)] for k in range(len(chunks))]
    own = project_last(upstream, out_weight, width, third)
    lent = send(mine, "ch", blocks, 1)

    before, pays, states, locs = [], [], [], []

    def take(chunk, low, high, sigp, y, y1):
        grad, z, own_state = gradient_states([own, lent, *chunk], high - low, low, dec, length)
        states.append(own_state)
        pays.append(filter_sums(grad, sigp, dec, y, y1, length, low))
        locs.append((grad, z, low))

    for hop in levels:
        if hop == levels[-1]:
            sent, own = lax.optimization_barrier((sent, own))
            pass
        there = send(sent, "ctx", groups, hop)
        if hop == 1:
            there, pairs = lax.optimization_barrier((there, pairs))
        if hop != levels[-1]:
            sent, after, *rest = prefix_step(
                place, there, state, before, dec, tokens, length, hop, hop * 2 != levels[-1]
            )
            state, before = (rest + [None])[0], [after]
    ends = there
    for k in range(len(pays), len(chunks)):
        pays, arrived[k] = lax.optimization_barrier((pays, arrived[k]))
        take(arrived[k], *chunks[k], *tables[k])
    sent, state = join_states(states, chunks)
    locs = [local_part(grad, z, dec, res, gain, length, low) for grad, z, low in locs]
    there = send(sent, "ctx", groups, levels[0])
    sent, state, later, sums = merge(
        place, there, state, ends, pays, dec, before, chunks, tokens, length, levels[0], levels[-1]
    )
    for hop in levels[1:]:
        there = send(sent, "ctx", groups, hop)
        if hop != levels[-1]:
            sent, later, sums, *state = tail_step(
                place, there, state, later, sums, dec, tokens, length, hop, hop * 2 != levels[-1]
            )
            state = state[0] if state else None
    moved, sums = sum_step(there, sums)
    out = finish(place, there, later, dec, res, locs, chunks, tokens, length, levels[-1])
    ores, odec, oskip = results(send(moved, "ctx", groups, levels[0]), sums, res, length)
    return (out, ores.T, odec.T, oskip[0])


def solution(mesh):
    placed = (P("ctx", "ch"), P("ctx", "ch"), P(None, "ch"), P("ch", None), P("ch", None), P("ch"))
    return jax.shard_map(
        body,
        mesh=mesh,
        in_specs=placed,
        out_specs=(P("ctx", "ch"), P("ch", None), P("ch", None), P("ch")),
        check_vma=False,
    )
```

```python
import functools
import math

import jax
import jax.numpy as jnp
from jax import lax
from jax.experimental import pallas as pl
from jax.experimental.pallas import tpu as pltpu
from jax.sharding import PartitionSpec as P

F32 = jnp.float32
BF16 = jnp.bfloat16
SUB = 16
HALF = 8
LANES = 128
VMEM_LIMIT = 12 * 1024 * 1024
PROJECT_LIMIT = 43 * 1024 * 1024
VM = pl.BlockSpec(memory_space=pltpu.VMEM)
SM = pl.BlockSpec(memory_space=pltpu.SMEM)
HBM = pl.BlockSpec(memory_space=pl.ANY)


def interleave(tokens, transpose=False):
    steps = tokens // SUB
    row = lax.broadcasted_iota(jnp.int32, (tokens, tokens), 1 if transpose else 0)
    col = lax.broadcasted_iota(jnp.int32, (tokens, tokens), 0 if transpose else 1)
    source = (row & (SUB - 1)) * steps + lax.shift_right_logical(row, SUB.bit_length() - 1)
    return jnp.where(col == source, 1.0, 0.0).astype(BF16)


def group_sums(groups, size):
    col = lax.broadcasted_iota(jnp.int32, (groups, groups * size), 1)
    row = lax.broadcasted_iota(jnp.int32, (groups, groups * size), 0)
    return jnp.where(lax.shift_right_logical(col, size.bit_length() - 1) == row, 1.0, 0.0).astype(F32)


def params(limit=VMEM_LIMIT):
    return pltpu.CompilerParams(vmem_limit_bytes=limit)


SMALL = pl.CostEstimate(flops=1, bytes_accessed=1, transcendentals=0)


def takes(microseconds):
    return pl.CostEstimate(flops=int(microseconds * 1e9), bytes_accessed=1, transcendentals=0)


def spread(row):
    return jnp.broadcast_to(row, (HALF, row.shape[-1]))


def pairwise(terms):
    while len(terms) > 1:
        rest = terms[len(terms) // 2 * 2 :]
        terms = [a + b for a, b in zip(terms[::2], terms[1::2])] + rest
    return terms[0]


def lane_block(block):
    return pl.ds(pl.multiple_of(block * LANES, LANES), LANES)


def rows_of(i, half):
    return pl.ds(SUB * i + HALF * half, HALF)


def recur(poles, values):
    last = values[-1]
    sums = [last] * len(poles)
    firsts = None
    for value in values[-2::-1]:
        if firsts is None:
            moved = [p * s for p, s in zip(poles, sums)]
            firsts = moved
        else:
            firsts = [p * (f + s) for p, f, s in zip(poles, firsts, sums)]
            moved = [p * s for p, s in zip(poles, sums)]
        sums = [m + value for m in moved]
    return sums, firsts


def signal_chunk(length, low, high, sig_ref, dec_ref, end_ref, sigp_ref, y_ref, y1_ref, ebuf, e1buf):
    tokens, width = sig_ref.shape[0], high - low
    modes = dec_ref.shape[0]
    steps = tokens // SUB
    sigp_ref[...] = jnp.dot(
        interleave(tokens), sig_ref[:, low:high], preferred_element_type=F32
    ).astype(BF16)

    @pl.loop(0, width // LANES)
    def _(block):
        lanes = lane_block(block)
        there = lane_block(block + low // LANES)
        rate = dec_ref[:, there] * (1.0 / length)
        pole_all = jnp.exp(-rate)
        pole_sub = jnp.exp(-rate * steps)
        both = [sigp_ref[pl.ds(SUB * i, SUB), lanes].astype(F32) for i in range(steps)]
        for half in range(2):
            values = [both[i][HALF * half : HALF * (half + 1)] for i in reversed(range(steps))]
            for first in range(0, modes, 8):
                poles = [spread(pole_all[n : n + 1]) for n in range(first, first + 8)]
                sums, firsts = recur(poles, values)
                for n in range(8):
                    rows = rows_of(first + n, half)
                    end = poles[n] * sums[n]
                    ebuf[rows, :] = end
                    e1buf[rows, :] = poles[n] * firsts[n] + end
        carry = jnp.zeros((modes, LANES), F32)
        carry1 = jnp.zeros((modes, LANES), F32)
        for j in range(SUB):
            pick = pl.ds(j, modes, stride=SUB)
            end, end1 = ebuf[pick, :], e1buf[pick, :]
            ebuf[pick, :] = carry
            e1buf[pick, :] = carry1
            carry1 = pole_sub * (carry1 + steps * carry) + end1
            carry = pole_sub * carry + end
        y_ref[:, lanes] = ebuf[...].astype(BF16)
        y1_ref[:, lanes] = e1buf[...].astype(BF16)
        end_ref[0:modes, there] = carry
        end_ref[modes : 2 * modes, there] = carry1


def gradient_kernel(length, base, parts, *refs):
    own_ref, lent_ref, *got_refs = refs[: 1 + parts]
    dec_ref, grad_ref, z_ref, state_ref, sbuf = refs[1 + parts :]
    tokens, width = grad_ref.shape
    modes = dec_ref.shape[0]
    steps = tokens // SUB
    place = lax.broadcasted_iota(jnp.int32, (HALF, LANES), 0).astype(F32) * steps
    total = own_ref[:, base : base + width].astype(F32)
    total = total + lent_ref[:, base : base + width].astype(F32)
    for got in got_refs:
        total = total + got[...].astype(F32)
    grad_ref[...] = jnp.dot(
        interleave(tokens), total.astype(BF16), preferred_element_type=F32
    )

    @pl.loop(0, width // LANES)
    def _(block):
        here = lane_block(block)
        rate = dec_ref[:, lane_block(block + base // LANES)] * (-1.0 / length)
        pole_all = jnp.exp(rate)
        for half in range(2):
            values = [grad_ref[rows_of(i, half), here] for i in range(steps)]
            for first in range(0, modes, 8):
                poles = [spread(pole_all[n : n + 1]) for n in range(first, first + 8)]
                sums = [values[-1]] * 8
                for value in values[-2::-1]:
                    sums = [p * v + value for p, v in zip(poles, sums)]
                for n in range(8):
                    out = pl.ds(HALF * (first + n), HALF)
                    reach = jnp.exp(spread(rate[first + n : first + n + 1]) * (place + half * HALF * steps))
                    moved = reach * sums[n]
                    z_ref[block, rows_of(first + n, half), :] = moved
                    sbuf[out, here] = moved if half == 0 else sbuf[out, here] + moved

    state_ref[...] = jnp.dot(group_sums(modes, HALF), sbuf[...], preferred_element_type=F32)


def gradient_states(pieces, width, base, decays, length):
    tokens = pieces[0].shape[0]
    modes = decays.shape[0]
    return pl.pallas_call(
        functools.partial(gradient_kernel, length, base, len(pieces) - 1),
        out_shape=(
            jax.ShapeDtypeStruct((tokens, width), F32),
            jax.ShapeDtypeStruct((width // LANES, modes * SUB, LANES), F32),
            jax.ShapeDtypeStruct((modes, width), F32),
        ),
        in_specs=[VM] * (len(pieces) + 1),
        out_specs=(VM,) * 3,
        scratch_shapes=[pltpu.VMEM((modes * HALF, width), F32)],
        compiler_params=params(),
        cost_estimate=takes(1),
        name="gradient_states",
    )(*pieces, decays)


def filter_kernel(length, base, grad_ref, sigp_ref, dec_ref, y_ref, y1_ref, pay_ref, s1buf, rbuf, dbuf, gf):
    tokens, width = grad_ref.shape
    modes = dec_ref.shape[0]
    steps = tokens // SUB
    place = lax.broadcasted_iota(jnp.int32, (HALF, LANES), 0).astype(F32) * steps

    @pl.loop(0, width // LANES)
    def _(block):
        here = lane_block(block)
        rate = dec_ref[:, lane_block(block + base // LANES)] * (-1.0 / length)
        pole_all = jnp.exp(rate)
        both = [sigp_ref[pl.ds(SUB * i, SUB), here].astype(F32) for i in range(steps)]
        for half in range(2):
            values = [grad_ref[rows_of(i, half), here] for i in range(steps)]
            for first in range(0, modes, 8):
                poles = [spread(pole_all[n : n + 1]) for n in range(first, first + 8)]
                sums, firsts = recur(poles, values)
                for n in range(8):
                    rows = rows_of(first + n, half)
                    out = pl.ds(HALF * (first + n), HALF)
                    before, before1 = y_ref[rows, here].astype(F32), y1_ref[rows, here].astype(F32)
                    ahead = place + half * HALF * steps
                    reach = jnp.exp(spread(rate[first + n : first + n + 1]) * ahead)
                    terms = (
                        (s1buf, reach * (firsts[n] + ahead * sums[n])),
                        (rbuf, sums[n] * before),
                        (dbuf, sums[n] * before1 + firsts[n] * before),
                    )
                    for ref, term in terms:
                        ref[out, here] = term if half == 0 else ref[out, here] + term
            seen = [v[HALF * half : HALF * (half + 1)] for v in both]
            for lag in range(steps):
                term = pairwise([values[i + lag] * seen[i] for i in range(steps - lag)])
                out = pl.ds(HALF * lag, HALF)
                gf[out, here] = term if half == 0 else gf[out, here] + term

    adder = group_sums(modes, HALF)
    add = lambda m, ref: jnp.dot(m, ref[...], preferred_element_type=F32)
    lags = add(group_sums(steps, HALF), gf)
    res, dec, first = add(adder, rbuf), add(adder, dbuf), add(adder, s1buf)
    pole = jnp.exp(dec_ref[:, base : base + width] * (-1.0 / length))
    res = res + lags[0:1]
    weight = pole
    for lag in range(1, steps):
        term = weight * lags[lag : lag + 1]
        res = res + term
        dec = dec + lag * term
        weight = weight * pole
    for k, rows in enumerate((res, dec, first)):
        pay_ref[k * modes : (k + 1) * modes, :] = rows
    pay_ref[3 * modes :, :] = jnp.broadcast_to(lags[0:1], (8, width))


def filter_sums(grad, sigp, decays, y, y1, length, base):
    tokens, width = grad.shape
    modes = decays.shape[0]
    buf = pltpu.VMEM((modes * HALF, width), F32)
    return pl.pallas_call(
        functools.partial(filter_kernel, length, base),
        out_shape=jax.ShapeDtypeStruct((3 * modes + 8, width), F32),
        in_specs=[VM] * 5,
        out_specs=VM,
        scratch_shapes=[buf] * 3 + [pltpu.VMEM((tokens // SUB * HALF, width), F32)],
        compiler_params=params(),
        cost_estimate=takes(3),
        name="filter_sums",
    )(grad, sigp, decays, y, y1)


def carry_out(outs, poles, starts):
    outs = list(outs)
    for i in reversed(range(len(outs))):
        outs[i] = outs[i] + pairwise(starts)
        if i:
            starts = [p * s for p, s in zip(poles, starts)]
    return outs


def local_kernel(length, base, grad_ref, z_ref, dec_ref, res_ref, gain_ref, loc_ref, cbuf, zbuf):
    tokens, width = grad_ref.shape
    modes = dec_ref.shape[0]
    steps = tokens // SUB

    @pl.loop(0, width // LANES)
    def _(block):
        here = lane_block(block)
        lanes = lane_block(block + base // LANES)
        rate = dec_ref[:, lanes] * (1.0 / length)
        pole_all = jnp.exp(-rate)
        weight = res_ref[:, lanes] * (1.0 / math.sqrt(length))
        gain = spread(gain_ref[:, lanes])
        zbuf[...] = z_ref[block]
        sums = jnp.zeros((modes, LANES), F32)
        for j in reversed(range(SUB)):
            pick = pl.ds(j, modes, stride=SUB)
            back = jnp.exp(rate * (steps * (j + 1) - 1))
            cbuf[pick, :] = weight * (back * sums)
            sums = sums + zbuf[pick, :]
        filt = []
        for _ in range(steps):
            filt.append(spread(jnp.sum(weight, axis=0, keepdims=True)))
            weight = weight * pole_all
        for half in range(2):
            values = [grad_ref[rows_of(i, half), here] for i in range(steps)]
            outs = [
                pairwise([filt[lag] * values[i + lag] for lag in range(steps - i)]) for i in range(steps)
            ]
            for first in range(0, modes, 8):
                picked = range(first, first + 8)
                poles = [spread(pole_all[n : n + 1]) for n in picked]
                outs = carry_out(outs, poles, [cbuf[rows_of(n, half), :] for n in picked])
            for i in range(steps):
                loc_ref[rows_of(i, half), here] = outs[i] + gain * values[i]


def local_part(grad, z, decays, residues, gain, length, base):
    tokens, width = grad.shape
    modes = decays.shape[0]
    return pl.pallas_call(
        functools.partial(local_kernel, length, base),
        out_shape=jax.ShapeDtypeStruct((tokens, width), F32),
        in_specs=[VM] * 5,
        out_specs=VM,
        scratch_shapes=[pltpu.VMEM((modes * SUB, LANES), F32)] * 2,
        compiler_params=params(),
        cost_estimate=takes(1.5),
        name="local_part",
    )(grad, z, decays, residues, gain)


def finish_kernel(length, hop, chunks, me_ref, there_ref, later_ref, dec_ref, res_ref, *refs):
    locs = refs[: len(chunks)]
    o_ref, vals, work = refs[len(chunks) :]
    tokens = o_ref.shape[0]
    modes = dec_ref.shape[0]
    steps = tokens // SUB
    scale = 1.0 / math.sqrt(length)
    ahead = (SUB - 1 - lax.broadcasted_iota(jnp.int32, (HALF, LANES), 0)).astype(F32) * steps
    vals[...] = later_step(
        me_ref, there_ref.at[0:modes, :], later_ref[...], dec_ref, length, tokens, hop
    )

    for loc_ref, (low, high) in zip(locs, chunks):
        @pl.loop(0, (high - low) // LANES)
        def _(block):
            here = lane_block(block)
            lanes = lane_block(block + low // LANES)
            rate = dec_ref[:, lanes] * (-1.0 / length)
            pole_all = jnp.exp(rate)
            lead = scale * res_ref[:, lanes] * pole_all * vals[:, lanes]
            for half in range(2):
                outs = [loc_ref[rows_of(i, half), here] for i in range(steps)]
                for first in range(0, modes, 8):
                    picked = range(first, first + 8)
                    poles = [spread(pole_all[n : n + 1]) for n in picked]
                    starts = [
                        spread(lead[n : n + 1]) * jnp.exp(spread(rate[n : n + 1]) * (ahead - half * HALF * steps))
                        for n in picked
                    ]
                    outs = carry_out(outs, poles, starts)
                for i in range(steps):
                    work[rows_of(i, half), lanes] = outs[i]

    o_ref[...] = jnp.dot(
        interleave(tokens, transpose=True), work[...].astype(BF16), preferred_element_type=F32
    ).astype(BF16)


def finish(me, there, later, decays, residues, locs, chunks, tokens, length, hop):
    modes, width = decays.shape
    return pl.pallas_call(
        functools.partial(finish_kernel, length, hop, chunks),
        out_shape=jax.ShapeDtypeStruct((tokens, width), BF16),
        in_specs=[SM] + [VM] * (4 + len(locs)),
        out_specs=VM,
        scratch_shapes=[pltpu.VMEM((modes, width), F32), pltpu.VMEM((tokens, width), F32)],
        compiler_params=params(),
        cost_estimate=takes(3),
        name="finish",
    )(me, there, later, decays, residues, *locs)


def place_bits(me_ref, hop):
    me = me_ref[0]
    return (me & (hop - 1)).astype(F32), (me & hop) != 0


def before_step(me_ref, there_ref, before_refs, dec_ref, length, tokens, hop):
    modes = dec_ref.shape[0]
    inside, upper = place_bits(me_ref, hop)
    reach = jnp.exp(dec_ref[...] * (-1.0 / length) * (inside * tokens))
    other, other1 = there_ref[0:modes, :].astype(F32), there_ref[modes : 2 * modes, :].astype(F32)
    before = jnp.where(upper, reach * other, 0.0)
    before1 = jnp.where(upper, reach * (other1 + (inside * tokens) * other), 0.0)
    for ref in before_refs:
        before = before + ref[0:modes, :]
        before1 = before1 + ref[modes : 2 * modes, :]
    return before, before1


def prefix_kernel(length, tokens, hop, carried, me_ref, there_ref, state_ref, *refs):
    refs, (sent_ref, after_ref, *next_ref) = refs[: 1 + carried], refs[1 + carried :]
    *before_refs, dec_ref = refs
    modes = dec_ref.shape[0]
    rows, rows1 = slice(0, modes), slice(modes, 2 * modes)
    after_ref[rows, :], after_ref[rows1, :] = before_step(
        me_ref, there_ref, before_refs, dec_ref, length, tokens, hop
    )
    other, other1 = there_ref[rows, :].astype(F32), there_ref[rows1, :].astype(F32)
    state, first = state_ref[rows, :], state_ref[rows1, :]
    _, upper = place_bits(me_ref, hop)
    span = jnp.exp(dec_ref[...] * (-1.0 / length) * (hop * tokens))
    late, early = jnp.where(upper, state, other), jnp.where(upper, other, state)
    late1, early1 = jnp.where(upper, first, other1), jnp.where(upper, other1, first)
    first = late1 + span * (early1 + (hop * tokens) * early)
    state = late + span * early
    for part, value in ((rows, state), (rows1, first)):
        for ref in next_ref:
            ref[part, :] = value
        sent_ref[part, :] = value.astype(BF16)


def later_step(me_ref, there_ref, later, dec_ref, length, tokens, hop):
    inside, upper = place_bits(me_ref, hop)
    reach = jnp.exp(dec_ref[...] * (-1.0 / length) * ((hop - 1 - inside) * tokens))
    return later + jnp.where(upper, 0.0, reach * there_ref[...].astype(F32))


def suffix_step(me_ref, other, state, dec_ref, length, tokens, hop):
    _, upper = place_bits(me_ref, hop)
    span = jnp.exp(dec_ref[...] * (-1.0 / length) * (hop * tokens))
    return jnp.where(upper, other, state) + span * jnp.where(upper, state, other)


def merge_kernel(
    length, tokens, hop, last, chunks, me_ref, there_ref, state_ref, ends_ref, *refs
):
    sent_ref, next_ref, later_ref, sums_ref = refs[-4:]
    pays, (dec_ref, *before_refs) = refs[: len(chunks)], refs[len(chunks) : -4]
    modes = dec_ref.shape[0]
    all_before, all_before1 = before_step(me_ref, ends_ref, before_refs, dec_ref, length, tokens, last)
    nothing = jnp.zeros_like(later_ref)
    later_ref[...] = later_step(me_ref, there_ref, nothing, dec_ref, length, tokens, hop)
    state = suffix_step(
        me_ref, there_ref[...].astype(F32), state_ref[...], dec_ref, length, tokens, hop
    )
    next_ref[...] = state
    sent_ref[0:modes, :] = state.astype(BF16)
    for pay_ref, (low, high) in zip(pays, chunks):
        res, dec, first = [pay_ref[k * modes : (k + 1) * modes, :] for k in range(3)]
        skip = pay_ref[3 * modes :, :]
        before, before1 = all_before[:, low:high], all_before1[:, low:high]
        start = state_ref[:, low:high]
        res = res + start * before
        dec = dec + first * before + start * before1
        for at, value in ((0, res), (modes, dec), (2 * modes, skip)):
            end = at + value.shape[0]
            sums_ref[at:end, low:high] = value
            sent_ref[modes + at : modes + end, low:high] = value.astype(BF16)


def merge(me, there, state, ends, pays, decays, before, chunks, tokens, length, hop, last):
    modes, width = decays.shape
    args = (there, state, ends, *pays, decays, *before)
    return pl.pallas_call(
        functools.partial(merge_kernel, length, tokens, hop, last, chunks),
        out_shape=tuple(
            jax.ShapeDtypeStruct((rows, width), dtype)
            for rows, dtype in ((3 * modes + 8, BF16), (modes, F32), (modes, F32), (2 * modes + 8, F32))
        ),
        in_specs=[SM] + [VM] * len(args),
        out_specs=(VM,) * 4,
        compiler_params=params(),
        cost_estimate=SMALL,
        name="merge",
    )(me, *args)


def tail_kernel(
    length, tokens, hop, me_ref, there_ref, state_ref, later_ref, sums_ref, dec_ref,
    sent_ref, after_ref, total_ref, *next_ref,
):
    modes = dec_ref.shape[0]
    there = there_ref.at[0:modes, :]
    after_ref[...] = later_step(me_ref, there, later_ref[...], dec_ref, length, tokens, hop)
    state = suffix_step(me_ref, there[...].astype(F32), state_ref[...], dec_ref, length, tokens, hop)
    if next_ref:
        next_ref[0][...] = state
    sent_ref[0:modes, :] = state.astype(BF16)
    sums = sums_ref[...] + there_ref[modes:, :].astype(F32)
    total_ref[...] = sums
    sent_ref[modes:, :] = sums.astype(BF16)


def tail_step(me, there, state, later, sums, decays, tokens, length, hop, more):
    args = (there, state, later, sums, decays)
    outs = (there, later, sums) + ((state,) if more else ())
    return pl.pallas_call(
        functools.partial(tail_kernel, length, tokens, hop),
        out_shape=tuple(jax.ShapeDtypeStruct(x.shape, x.dtype) for x in outs),
        in_specs=[SM] + [VM] * 5,
        out_specs=(VM,) * len(outs),
        compiler_params=params(),
        cost_estimate=SMALL,
        name="tail_step",
    )(me, *args)


def sum_kernel(there_ref, sums_ref, sent_ref, total_ref):
    sums = sums_ref[...] + there_ref[there_ref.shape[0] - sums_ref.shape[0] :, :].astype(F32)
    total_ref[...] = sums
    sent_ref[...] = sums.astype(BF16)


def sum_step(there, sums):
    return pl.pallas_call(
        sum_kernel,
        out_shape=(jax.ShapeDtypeStruct(sums.shape, BF16), jax.ShapeDtypeStruct(sums.shape, F32)),
        in_specs=[VM] * 2,
        out_specs=(VM,) * 2,
        compiler_params=params(),
        cost_estimate=SMALL,
        name="sum_step",
    )(there, sums)


def result_kernel(length, there_ref, sums_ref, res_ref, ores_ref, odec_ref, oskip_ref):
    modes = res_ref.shape[0]
    sums = sums_ref[...] + there_ref[...].astype(F32)
    ores_ref[...] = sums[0:modes] * (1.0 / length)
    odec_ref[...] = sums[modes : 2 * modes] * (-1.0 / (length * length)) * res_ref[...]
    oskip_ref[...] = sums[2 * modes : 2 * modes + 1] * (1.0 / math.sqrt(length))


def results(there, sums, residues, length):
    modes, width = residues.shape
    return pl.pallas_call(
        functools.partial(result_kernel, length),
        out_shape=(
            jax.ShapeDtypeStruct((modes, width), F32),
            jax.ShapeDtypeStruct((modes, width), F32),
            jax.ShapeDtypeStruct((1, width), F32),
        ),
        in_specs=[VM] * 3,
        out_specs=(VM,) * 3,
        compiler_params=params(),
        cost_estimate=SMALL,
        name="results",
    )(there, sums, residues)


def prefix_step(me, there, state, carried, decays, tokens, length, hop, more):
    args = [there, state, *carried, decays]
    dtypes = (BF16, F32, F32) if more else (BF16, F32)
    return pl.pallas_call(
        functools.partial(prefix_kernel, length, tokens, hop, len(carried)),
        out_shape=tuple(jax.ShapeDtypeStruct(state.shape, dtype) for dtype in dtypes),
        in_specs=[SM] + [VM] * len(args),
        out_specs=(VM,) * len(dtypes),
        compiler_params=params(),
        cost_estimate=SMALL,
        name="prefix_step",
    )(me, *args)


def join_kernel(chunks, *refs):
    sent_ref, state_ref = refs[len(chunks) :]
    for part_ref, (low, high) in zip(refs, chunks):
        state_ref[:, low:high] = part_ref[...]
        sent_ref[:, low:high] = part_ref[...].astype(BF16)


def join_states(states, chunks):
    modes, width = states[0].shape[0], chunks[-1][1]
    return pl.pallas_call(
        functools.partial(join_kernel, chunks),
        out_shape=tuple(jax.ShapeDtypeStruct((modes, width), dtype) for dtype in (BF16, F32)),
        in_specs=[VM] * len(states),
        out_specs=(VM,) * 2,
        compiler_params=params(),
        cost_estimate=SMALL,
        name="join_states",
    )(*states)


def weight_copies(blocks_ref, w_ref, width, targets, sems):
    copies = []
    for q, target in enumerate(targets):
        start = pl.multiple_of(blocks_ref[q] * width, width)
        copies.append(pltpu.make_async_copy(w_ref.at[pl.ds(start, width)], target, sems.at[q]))
    return copies


def project_block(up_ref, w_rows, out_ref):
    width = w_rows.shape[0]
    rows = min(width, 256)
    for start in range(0, width, rows):
        out_ref[:, start : start + rows] = lax.dot_general(
            up_ref[...], w_rows[start : start + rows, :], (((1,), (1,)), ((), ())),
            preferred_element_type=F32,
        ).astype(out_ref.dtype)


def fetch_kernel(blocks_ref, w_ref, o_ref, sems):
    pieces = blocks_ref.shape[0]
    width = o_ref.shape[0] // pieces
    targets = [o_ref.at[q * width : (q + 1) * width, :] for q in range(pieces)]
    copies = weight_copies(blocks_ref, w_ref, width, targets, sems)
    for copy in copies:
        copy.start()
    for copy in copies:
        copy.wait()


def fetch(weight, width, blocks):
    pieces = blocks.shape[0]
    return pl.pallas_call(
        fetch_kernel,
        out_shape=jax.ShapeDtypeStruct((pieces * width, weight.shape[1]), BF16),
        in_specs=[SM, HBM],
        out_specs=VM,
        scratch_shapes=[pltpu.SemaphoreType.DMA((pieces,))],
        compiler_params=params(PROJECT_LIMIT),
        cost_estimate=takes(3),
        name="fetch",
    )(blocks, weight)


def multiply_kernel(up_ref, held_ref, o_ref):
    project_block(up_ref, held_ref, o_ref)


def multiply(up, held):
    return pl.pallas_call(
        multiply_kernel,
        out_shape=jax.ShapeDtypeStruct((up.shape[0], held.shape[0]), BF16),
        in_specs=[VM] * 2,
        out_specs=VM,
        compiler_params=params(),
        cost_estimate=takes(1),
        name="multiply",
    )(up, held)


def scan_kernel(pieces, chunks, length, blocks_ref, up_ref, w_ref, sig_ref, dec_ref, *refs):
    outs, (end_ref, sent_ref, *tables) = refs[:pieces], refs[pieces:-4]
    w_buf, sems, ebuf, e1buf = refs[-4:]
    width = w_buf.shape[1]
    copies = weight_copies(blocks_ref, w_ref, width, [w_buf.at[q] for q in range(pieces)], sems)
    for copy in copies:
        copy.start()
    for k, (low, high) in enumerate(chunks):
        signal_chunk(length, low, high, sig_ref, dec_ref, end_ref, *tables[3 * k : 3 * k + 3], ebuf, e1buf)
    sent_ref[...] = end_ref[...].astype(BF16)
    for copy in copies:
        copy.wait()
    for q, out in enumerate(outs):
        project_block(up_ref, w_buf.at[q], out)


def project_and_scan(up, weight, width, blocks, signal, decays, chunks, length):
    tokens, feats = up.shape
    modes = decays.shape[0]
    pieces = blocks.shape[0]
    shapes = [jax.ShapeDtypeStruct((tokens, width), BF16)] * pieces
    shapes += [jax.ShapeDtypeStruct((2 * modes, width), dtype) for dtype in (F32, BF16)]
    for low, high in chunks:
        states = jax.ShapeDtypeStruct((modes * SUB, high - low), BF16)
        shapes += [jax.ShapeDtypeStruct((tokens, high - low), BF16), states, states]
    out = pl.pallas_call(
        functools.partial(scan_kernel, pieces, chunks, length),
        out_shape=shapes,
        in_specs=[SM, VM, HBM, VM, VM],
        out_specs=[VM] * len(shapes),
        scratch_shapes=[
            pltpu.VMEM((pieces, width, feats), BF16),
            pltpu.SemaphoreType.DMA((pieces,)),
        ]
        + [pltpu.VMEM((modes * SUB, LANES), F32)] * 2,
        compiler_params=params(PROJECT_LIMIT),
        cost_estimate=takes(6),
        name="project_and_scan",
    )(blocks, up, weight, signal, decays)
    tables = out[pieces + 2 :]
    return out[:pieces], out[pieces : pieces + 2], [
        tables[3 * k : 3 * k + 3] for k in range(len(chunks))
    ]


def last_kernel(block_ref, up_ref, w_ref, o_ref, w_buf, sems):
    (copy,) = weight_copies(block_ref, w_ref, w_buf.shape[0], [w_buf], sems)
    copy.start()
    copy.wait()
    project_block(up_ref, w_buf, o_ref)


def project_last(up, weight, width, block):
    tokens, feats = up.shape
    return pl.pallas_call(
        last_kernel,
        out_shape=jax.ShapeDtypeStruct((tokens, width), BF16),
        in_specs=[SM, VM, HBM],
        out_specs=VM,
        scratch_shapes=[pltpu.VMEM((width, feats), BF16), pltpu.SemaphoreType.DMA((1,))],
        compiler_params=params(PROJECT_LIMIT),
        cost_estimate=takes(4),
        name="project_last",
    )(block, up, weight)


def pair_kernel(chunks, lent, mine_ref, lent_ref, *outs):
    base = mine_ref.shape[1] * lent
    for (low, high), out in zip(chunks, outs):
        total = mine_ref[:, low:high].astype(F32) + lent_ref[:, base + low : base + high].astype(F32)
        out[...] = total.astype(BF16)


def pair_sums(mine, lent, index, chunks):
    tokens = mine.shape[0]
    return pl.pallas_call(
        functools.partial(pair_kernel, chunks, index),
        out_shape=[jax.ShapeDtypeStruct((tokens, high - low), BF16) for low, high in chunks],
        in_specs=[VM] * 2,
        out_specs=[VM] * len(chunks),
        compiler_params=params(),
        cost_estimate=SMALL,
        name="pair_sums",
    )(mine, lent)


def send(x, axis, size, hop):
    return lax.ppermute(x, axis, [(i, i ^ hop) for i in range(size)])


def cuts(width):
    lane_blocks = width // LANES
    first = lane_blocks // 2 * LANES
    return [(0, first), (first, width)]


def body(signal, upstream, out_weight, residues, decays, skip_gain):
    tokens, width = signal.shape
    groups = lax.axis_size("ctx")
    blocks = lax.axis_size("ch")
    length = tokens * groups
    modes = residues.shape[1]
    me = lax.axis_index("ch")
    place = jnp.reshape(lax.axis_index("ctx").astype(jnp.int32), (1,))
    dec = decays.T
    res = residues.T
    gain = skip_gain[None, :]
    chunks = cuts(width)
    hops = range(2, blocks, 2)
    levels = [1 << k for k in range(groups.bit_length() - 1)]

    index = lambda blocks: jnp.stack(blocks).astype(jnp.int32)
    first, second, third = index([me ^ hop ^ 1 for hop in hops]), index([me ^ hop for hop in hops] + [me ^ 1]), index([me])
    first, second, third, place = lax.optimization_barrier((first, second, third, place))
    lent = send(multiply(upstream, fetch(out_weight, width, first)), "ch", blocks, 1)
    (*parts, mine), (state, sent), tables = project_and_scan(
        upstream, out_weight, width, second, signal, dec, chunks, length
    )
    pairs = [pair_sums(part, lent, index, chunks) for index, part in enumerate(parts)]
    upstream, pairs = lax.optimization_barrier((upstream, pairs))
    arrived = [[send(pair[k], "ch", blocks, hop) for pair, hop in zip(pairs, hops)] for k in range(len(chunks))]
    own = project_last(upstream, out_weight, width, third)
    lent = send(mine, "ch", blocks, 1)

    before, pays, states, locs = [], [], [], []

    def take(chunk, low, high, sigp, y, y1):
        grad, z, own_state = gradient_states([own, lent, *chunk], high - low, low, dec, length)
        states.append(own_state)
        pays.append(filter_sums(grad, sigp, dec, y, y1, length, low))
        locs.append((grad, z, low))

    for hop in levels:
        if hop == levels[-1]:
            sent, own = lax.optimization_barrier((sent, own))
            pass
        there = send(sent, "ctx", groups, hop)
        if hop == 1:
            there, pairs = lax.optimization_barrier((there, pairs))
        if hop != levels[-1]:
            sent, after, *rest = prefix_step(
                place, there, state, before, dec, tokens, length, hop, hop * 2 != levels[-1]
            )
            state, before = (rest + [None])[0], [after]
    ends = there
    for k in range(len(pays), len(chunks)):
        pays, arrived[k] = lax.optimization_barrier((pays, arrived[k]))
        take(arrived[k], *chunks[k], *tables[k])
    sent, state = join_states(states, chunks)
    locs = [local_part(grad, z, dec, res, gain, length, low) for grad, z, low in locs]
    there = send(sent, "ctx", groups, levels[0])
    sent, state, later, sums = merge(
        place, there, state, ends, pays, dec, before, chunks, tokens, length, levels[0], levels[-1]
    )
    for hop in levels[1:]:
        there = send(sent, "ctx", groups, hop)
        if hop != levels[-1]:
            sent, later, sums, *state = tail_step(
                place, there, state, later, sums, dec, tokens, length, hop, hop * 2 != levels[-1]
            )
            state = state[0] if state else None
    moved, sums = sum_step(there, sums)
    out = finish(place, there, later, dec, res, locs, chunks, tokens, length, levels[-1])
    ores, odec, oskip = results(send(moved, "ctx", groups, levels[0]), sums, res, length)
    return (out, ores.T, odec.T, oskip[0])


def solution(mesh):
    placed = (P("ctx", "ch"), P("ctx", "ch"), P(None, "ch"), P("ch", None), P("ch", None), P("ch"))
    return jax.shard_map(
        body,
        mesh=mesh,
        in_specs=placed,
        out_specs=(P("ctx", "ch"), P("ch", None), P("ch", None), P("ch")),
        check_vma=False,
    )
```

```python
import functools
import math

import jax
import jax.numpy as jnp
from jax import lax
from jax.experimental import pallas as pl
from jax.experimental.pallas import tpu as pltpu
from jax.sharding import PartitionSpec as P

F32 = jnp.float32
BF16 = jnp.bfloat16
SUB = 16
HALF = 8
LANES = 128
VMEM_LIMIT = 12 * 1024 * 1024
PROJECT_LIMIT = 43 * 1024 * 1024
VM = pl.BlockSpec(memory_space=pltpu.VMEM)
SM = pl.BlockSpec(memory_space=pltpu.SMEM)
HBM = pl.BlockSpec(memory_space=pl.ANY)


def interleave(tokens, transpose=False):
    steps = tokens // SUB
    row = lax.broadcasted_iota(jnp.int32, (tokens, tokens), 1 if transpose else 0)
    col = lax.broadcasted_iota(jnp.int32, (tokens, tokens), 0 if transpose else 1)
    source = (row & (SUB - 1)) * steps + lax.shift_right_logical(row, SUB.bit_length() - 1)
    return jnp.where(col == source, 1.0, 0.0).astype(BF16)


def group_sums(groups, size):
    col = lax.broadcasted_iota(jnp.int32, (groups, groups * size), 1)
    row = lax.broadcasted_iota(jnp.int32, (groups, groups * size), 0)
    return jnp.where(lax.shift_right_logical(col, size.bit_length() - 1) == row, 1.0, 0.0).astype(F32)


def params(limit=VMEM_LIMIT):
    return pltpu.CompilerParams(vmem_limit_bytes=limit)


SMALL = pl.CostEstimate(flops=1, bytes_accessed=1, transcendentals=0)


def takes(microseconds):
    return pl.CostEstimate(flops=int(microseconds * 1e9), bytes_accessed=1, transcendentals=0)


def spread(row):
    return jnp.broadcast_to(row, (HALF, row.shape[-1]))


def pairwise(terms):
    while len(terms) > 1:
        rest = terms[len(terms) // 2 * 2 :]
        terms = [a + b for a, b in zip(terms[::2], terms[1::2])] + rest
    return terms[0]


def lane_block(block):
    return pl.ds(pl.multiple_of(block * LANES, LANES), LANES)


def rows_of(i, half):
    return pl.ds(SUB * i + HALF * half, HALF)


def recur(poles, values):
    last = values[-1]
    sums = [last] * len(poles)
    firsts = None
    for value in values[-2::-1]:
        if firsts is None:
            moved = [p * s for p, s in zip(poles, sums)]
            firsts = moved
        else:
            firsts = [p * (f + s) for p, f, s in zip(poles, firsts, sums)]
            moved = [p * s for p, s in zip(poles, sums)]
        sums = [m + value for m in moved]
    return sums, firsts


def signal_chunk(length, low, high, sig_ref, dec_ref, end_ref, sigp_ref, y_ref, y1_ref, ebuf, e1buf):
    tokens, width = sig_ref.shape[0], high - low
    modes = dec_ref.shape[0]
    steps = tokens // SUB
    sigp_ref[...] = jnp.dot(
        interleave(tokens), sig_ref[:, low:high], preferred_element_type=F32
    ).astype(BF16)

    @pl.loop(0, width // LANES)
    def _(block):
        lanes = lane_block(block)
        there = lane_block(block + low // LANES)
        rate = dec_ref[:, there] * (1.0 / length)
        pole_all = jnp.exp(-rate)
        pole_sub = jnp.exp(-rate * steps)
        both = [sigp_ref[pl.ds(SUB * i, SUB), lanes].astype(F32) for i in range(steps)]
        for half in range(2):
            values = [both[i][HALF * half : HALF * (half + 1)] for i in reversed(range(steps))]
            for first in range(0, modes, 8):
                poles = [spread(pole_all[n : n + 1]) for n in range(first, first + 8)]
                sums, firsts = recur(poles, values)
                for n in range(8):
                    rows = rows_of(first + n, half)
                    end = poles[n] * sums[n]
                    ebuf[rows, :] = end
                    e1buf[rows, :] = poles[n] * firsts[n] + end
        carry = jnp.zeros((modes, LANES), F32)
        carry1 = jnp.zeros((modes, LANES), F32)
        for j in range(SUB):
            pick = pl.ds(j, modes, stride=SUB)
            end, end1 = ebuf[pick, :], e1buf[pick, :]
            ebuf[pick, :] = carry
            e1buf[pick, :] = carry1
            carry1 = pole_sub * (carry1 + steps * carry) + end1
            carry = pole_sub * carry + end
        y_ref[:, lanes] = ebuf[...].astype(BF16)
        y1_ref[:, lanes] = e1buf[...].astype(BF16)
        end_ref[0:modes, there] = carry
        end_ref[modes : 2 * modes, there] = carry1


def gradient_kernel(length, base, parts, *refs):
    own_ref, lent_ref, *got_refs = refs[: 1 + parts]
    dec_ref, grad_ref, z_ref, state_ref, sbuf = refs[1 + parts :]
    tokens, width = grad_ref.shape
    modes = dec_ref.shape[0]
    steps = tokens // SUB
    place = lax.broadcasted_iota(jnp.int32, (HALF, LANES), 0).astype(F32) * steps
    total = own_ref[:, base : base + width].astype(F32)
    total = total + lent_ref[:, base : base + width].astype(F32)
    for got in got_refs:
        total = total + got[...].astype(F32)
    grad_ref[...] = jnp.dot(
        interleave(tokens), total.astype(BF16), preferred_element_type=F32
    )

    @pl.loop(0, width // LANES)
    def _(block):
        here = lane_block(block)
        rate = dec_ref[:, lane_block(block + base // LANES)] * (-1.0 / length)
        pole_all = jnp.exp(rate)
        for half in range(2):
            values = [grad_ref[rows_of(i, half), here] for i in range(steps)]
            for first in range(0, modes, 8):
                poles = [spread(pole_all[n : n + 1]) for n in range(first, first + 8)]
                sums = [values[-1]] * 8
                for value in values[-2::-1]:
                    sums = [p * v + value for p, v in zip(poles, sums)]
                for n in range(8):
                    out = pl.ds(HALF * (first + n), HALF)
                    reach = jnp.exp(spread(rate[first + n : first + n + 1]) * (place + half * HALF * steps))
                    moved = reach * sums[n]
                    z_ref[block, rows_of(first + n, half), :] = moved
                    sbuf[out, here] = moved if half == 0 else sbuf[out, here] + moved

    state_ref[...] = jnp.dot(group_sums(modes, HALF), sbuf[...], preferred_element_type=F32)


def gradient_states(pieces, width, base, decays, length):
    tokens = pieces[0].shape[0]
    modes = decays.shape[0]
    return pl.pallas_call(
        functools.partial(gradient_kernel, length, base, len(pieces) - 1),
        out_shape=(
            jax.ShapeDtypeStruct((tokens, width), F32),
            jax.ShapeDtypeStruct((width // LANES, modes * SUB, LANES), F32),
            jax.ShapeDtypeStruct((modes, width), F32),
        ),
        in_specs=[VM] * (len(pieces) + 1),
        out_specs=(VM,) * 3,
        scratch_shapes=[pltpu.VMEM((modes * HALF, width), F32)],
        compiler_params=params(),
        cost_estimate=takes(1),
        name="gradient_states",
    )(*pieces, decays)


def filter_kernel(length, base, grad_ref, sigp_ref, dec_ref, y_ref, y1_ref, pay_ref, s1buf, rbuf, dbuf, gf):
    tokens, width = grad_ref.shape
    modes = dec_ref.shape[0]
    steps = tokens // SUB
    place = lax.broadcasted_iota(jnp.int32, (HALF, LANES), 0).astype(F32) * steps

    @pl.loop(0, width // LANES)
    def _(block):
        here = lane_block(block)
        rate = dec_ref[:, lane_block(block + base // LANES)] * (-1.0 / length)
        pole_all = jnp.exp(rate)
        both = [sigp_ref[pl.ds(SUB * i, SUB), here].astype(F32) for i in range(steps)]
        for half in range(2):
            values = [grad_ref[rows_of(i, half), here] for i in range(steps)]
            for first in range(0, modes, 8):
                poles = [spread(pole_all[n : n + 1]) for n in range(first, first + 8)]
                sums, firsts = recur(poles, values)
                for n in range(8):
                    rows = rows_of(first + n, half)
                    out = pl.ds(HALF * (first + n), HALF)
                    before, before1 = y_ref[rows, here].astype(F32), y1_ref[rows, here].astype(F32)
                    ahead = place + half * HALF * steps
                    reach = jnp.exp(spread(rate[first + n : first + n + 1]) * ahead)
                    terms = (
                        (s1buf, reach * (firsts[n] + ahead * sums[n])),
                        (rbuf, sums[n] * before),
                        (dbuf, sums[n] * before1 + firsts[n] * before),
                    )
                    for ref, term in terms:
                        ref[out, here] = term if half == 0 else ref[out, here] + term
            seen = [v[HALF * half : HALF * (half + 1)] for v in both]
            for lag in range(steps):
                term = pairwise([values[i + lag] * seen[i] for i in range(steps - lag)])
                out = pl.ds(HALF * lag, HALF)
                gf[out, here] = term if half == 0 else gf[out, here] + term

    adder = group_sums(modes, HALF)
    add = lambda m, ref: jnp.dot(m, ref[...], preferred_element_type=F32)
    lags = add(group_sums(steps, HALF), gf)
    res, dec, first = add(adder, rbuf), add(adder, dbuf), add(adder, s1buf)
    pole = jnp.exp(dec_ref[:, base : base + width] * (-1.0 / length))
    res = res + lags[0:1]
    weight = pole
    for lag in range(1, steps):
        term = weight * lags[lag : lag + 1]
        res = res + term
        dec = dec + lag * term
        weight = weight * pole
    for k, rows in enumerate((res, dec, first)):
        pay_ref[k * modes : (k + 1) * modes, :] = rows
    pay_ref[3 * modes :, :] = jnp.broadcast_to(lags[0:1], (8, width))


def filter_sums(grad, sigp, decays, y, y1, length, base):
    tokens, width = grad.shape
    modes = decays.shape[0]
    buf = pltpu.VMEM((modes * HALF, width), F32)
    return pl.pallas_call(
        functools.partial(filter_kernel, length, base),
        out_shape=jax.ShapeDtypeStruct((3 * modes + 8, width), F32),
        in_specs=[VM] * 5,
        out_specs=VM,
        scratch_shapes=[buf] * 3 + [pltpu.VMEM((tokens // SUB * HALF, width), F32)],
        compiler_params=params(),
        cost_estimate=takes(3),
        name="filter_sums",
    )(grad, sigp, decays, y, y1)


def carry_out(outs, poles, starts):
    outs = list(outs)
    for i in reversed(range(len(outs))):
        outs[i] = outs[i] + pairwise(starts)
        if i:
            starts = [p * s for p, s in zip(poles, starts)]
    return outs


def local_kernel(length, base, grad_ref, z_ref, dec_ref, res_ref, gain_ref, loc_ref, reach_ref, cbuf, zbuf):
    tokens, width = grad_ref.shape
    modes = dec_ref.shape[0]
    steps = tokens // SUB
    ahead = (SUB - 1 - lax.broadcasted_iota(jnp.int32, (HALF, LANES), 0)).astype(F32) * steps

    @pl.loop(0, width // LANES)
    def _(block):
        here = lane_block(block)
        lanes = lane_block(block + base // LANES)
        rate = dec_ref[:, lanes] * (1.0 / length)
        pole_all = jnp.exp(-rate)
        weight = res_ref[:, lanes] * (1.0 / math.sqrt(length))
        gain = spread(gain_ref[:, lanes])
        zbuf[...] = z_ref[block]
        lead = weight * pole_all
        for n in range(modes):
            for half in range(2):
                left = ahead - half * HALF * steps
                reach_ref[rows_of(n, half), here] = spread(lead[n : n + 1]) * jnp.exp(
                    spread(-rate[n : n + 1]) * left
                )
        sums = jnp.zeros((modes, LANES), F32)
        for j in reversed(range(SUB)):
            pick = pl.ds(j, modes, stride=SUB)
            back = jnp.exp(rate * (steps * (j + 1) - 1))
            cbuf[pick, :] = weight * (back * sums)
            sums = sums + zbuf[pick, :]
        filt = []
        for _ in range(steps):
            filt.append(spread(jnp.sum(weight, axis=0, keepdims=True)))
            weight = weight * pole_all
        for half in range(2):
            values = [grad_ref[rows_of(i, half), here] for i in range(steps)]
            outs = [
                pairwise([filt[lag] * values[i + lag] for lag in range(steps - i)]) for i in range(steps)
            ]
            for first in range(0, modes, 8):
                picked = range(first, first + 8)
                poles = [spread(pole_all[n : n + 1]) for n in picked]
                outs = carry_out(outs, poles, [cbuf[rows_of(n, half), :] for n in picked])
            for i in range(steps):
                loc_ref[rows_of(i, half), here] = outs[i] + gain * values[i]


def local_part(grad, z, decays, residues, gain, length, base):
    tokens, width = grad.shape
    modes = decays.shape[0]
    return pl.pallas_call(
        functools.partial(local_kernel, length, base),
        out_shape=(
            jax.ShapeDtypeStruct((tokens, width), F32),
            jax.ShapeDtypeStruct((modes * SUB, width), F32),
        ),
        in_specs=[VM] * 5,
        out_specs=(VM,) * 2,
        scratch_shapes=[pltpu.VMEM((modes * SUB, LANES), F32)] * 2,
        compiler_params=params(),
        cost_estimate=takes(1.5),
        name="local_part",
    )(grad, z, decays, residues, gain)


def finish_kernel(length, hop, chunks, me_ref, there_ref, later_ref, dec_ref, *refs):
    locs, reaches = refs[: len(chunks)], refs[len(chunks) : 2 * len(chunks)]
    o_ref, vals, work = refs[2 * len(chunks) :]
    tokens = o_ref.shape[0]
    modes = dec_ref.shape[0]
    steps = tokens // SUB
    vals[...] = later_step(
        me_ref, there_ref.at[0:modes, :], later_ref[...], dec_ref, length, tokens, hop
    )

    for loc_ref, reach_ref, (low, high) in zip(locs, reaches, chunks):
        @pl.loop(0, (high - low) // LANES)
        def _(block):
            here = lane_block(block)
            lanes = lane_block(block + low // LANES)
            pole_all = jnp.exp(dec_ref[:, lanes] * (-1.0 / length))
            later = vals[:, lanes]
            for half in range(2):
                outs = [loc_ref[rows_of(i, half), here] for i in range(steps)]
                for first in range(0, modes, 8):
                    picked = range(first, first + 8)
                    poles = [spread(pole_all[n : n + 1]) for n in picked]
                    starts = [spread(later[n : n + 1]) * reach_ref[rows_of(n, half), here] for n in picked]
                    outs = carry_out(outs, poles, starts)
                for i in range(steps):
                    work[rows_of(i, half), lanes] = outs[i]

    o_ref[...] = jnp.dot(
        interleave(tokens, transpose=True), work[...].astype(BF16), preferred_element_type=F32
    ).astype(BF16)


def finish(me, there, later, decays, locs, reaches, chunks, tokens, length, hop):
    modes, width = decays.shape
    return pl.pallas_call(
        functools.partial(finish_kernel, length, hop, chunks),
        out_shape=jax.ShapeDtypeStruct((tokens, width), BF16),
        in_specs=[SM] + [VM] * (3 + 2 * len(locs)),
        out_specs=VM,
        scratch_shapes=[pltpu.VMEM((modes, width), F32), pltpu.VMEM((tokens, width), F32)],
        compiler_params=params(),
        cost_estimate=takes(3),
        name="finish",
    )(me, there, later, decays, *locs, *reaches)


def place_bits(me_ref, hop):
    me = me_ref[0]
    return (me & (hop - 1)).astype(F32), (me & hop) != 0


def before_step(me_ref, there_ref, before_refs, dec_ref, length, tokens, hop):
    modes = dec_ref.shape[0]
    inside, upper = place_bits(me_ref, hop)
    reach = jnp.exp(dec_ref[...] * (-1.0 / length) * (inside * tokens))
    other, other1 = there_ref[0:modes, :].astype(F32), there_ref[modes : 2 * modes, :].astype(F32)
    before = jnp.where(upper, reach * other, 0.0)
    before1 = jnp.where(upper, reach * (other1 + (inside * tokens) * other), 0.0)
    for ref in before_refs:
        before = before + ref[0:modes, :]
        before1 = before1 + ref[modes : 2 * modes, :]
    return before, before1


def prefix_kernel(length, tokens, hop, carried, me_ref, there_ref, state_ref, *refs):
    refs, (sent_ref, after_ref, *next_ref) = refs[: 1 + carried], refs[1 + carried :]
    *before_refs, dec_ref = refs
    modes = dec_ref.shape[0]
    rows, rows1 = slice(0, modes), slice(modes, 2 * modes)
    after_ref[rows, :], after_ref[rows1, :] = before_step(
        me_ref, there_ref, before_refs, dec_ref, length, tokens, hop
    )
    other, other1 = there_ref[rows, :].astype(F32), there_ref[rows1, :].astype(F32)
    state, first = state_ref[rows, :], state_ref[rows1, :]
    _, upper = place_bits(me_ref, hop)
    span = jnp.exp(dec_ref[...] * (-1.0 / length) * (hop * tokens))
    late, early = jnp.where(upper, state, other), jnp.where(upper, other, state)
    late1, early1 = jnp.where(upper, first, other1), jnp.where(upper, other1, first)
    first = late1 + span * (early1 + (hop * tokens) * early)
    state = late + span * early
    for part, value in ((rows, state), (rows1, first)):
        for ref in next_ref:
            ref[part, :] = value
        sent_ref[part, :] = value.astype(BF16)


def later_step(me_ref, there_ref, later, dec_ref, length, tokens, hop):
    inside, upper = place_bits(me_ref, hop)
    reach = jnp.exp(dec_ref[...] * (-1.0 / length) * ((hop - 1 - inside) * tokens))
    return later + jnp.where(upper, 0.0, reach * there_ref[...].astype(F32))


def suffix_step(me_ref, other, state, dec_ref, length, tokens, hop):
    _, upper = place_bits(me_ref, hop)
    span = jnp.exp(dec_ref[...] * (-1.0 / length) * (hop * tokens))
    return jnp.where(upper, other, state) + span * jnp.where(upper, state, other)


def merge_kernel(
    length, tokens, hop, last, chunks, me_ref, there_ref, state_ref, ends_ref, *refs
):
    sent_ref, next_ref, later_ref, sums_ref = refs[-4:]
    pays, (dec_ref, *before_refs) = refs[: len(chunks)], refs[len(chunks) : -4]
    modes = dec_ref.shape[0]
    all_before, all_before1 = before_step(me_ref, ends_ref, before_refs, dec_ref, length, tokens, last)
    nothing = jnp.zeros_like(later_ref)
    later_ref[...] = later_step(me_ref, there_ref, nothing, dec_ref, length, tokens, hop)
    state = suffix_step(
        me_ref, there_ref[...].astype(F32), state_ref[...], dec_ref, length, tokens, hop
    )
    next_ref[...] = state
    sent_ref[0:modes, :] = state.astype(BF16)
    for pay_ref, (low, high) in zip(pays, chunks):
        res, dec, first = [pay_ref[k * modes : (k + 1) * modes, :] for k in range(3)]
        skip = pay_ref[3 * modes :, :]
        before, before1 = all_before[:, low:high], all_before1[:, low:high]
        start = state_ref[:, low:high]
        res = res + start * before
        dec = dec + first * before + start * before1
        for at, value in ((0, res), (modes, dec), (2 * modes, skip)):
            end = at + value.shape[0]
            sums_ref[at:end, low:high] = value
            sent_ref[modes + at : modes + end, low:high] = value.astype(BF16)


def merge(me, there, state, ends, pays, decays, before, chunks, tokens, length, hop, last):
    modes, width = decays.shape
    args = (there, state, ends, *pays, decays, *before)
    return pl.pallas_call(
        functools.partial(merge_kernel, length, tokens, hop, last, chunks),
        out_shape=tuple(
            jax.ShapeDtypeStruct((rows, width), dtype)
            for rows, dtype in ((3 * modes + 8, BF16), (modes, F32), (modes, F32), (2 * modes + 8, F32))
        ),
        in_specs=[SM] + [VM] * len(args),
        out_specs=(VM,) * 4,
        compiler_params=params(),
        cost_estimate=SMALL,
        name="merge",
    )(me, *args)


def tail_kernel(
    length, tokens, hop, me_ref, there_ref, state_ref, later_ref, sums_ref, dec_ref,
    sent_ref, after_ref, total_ref, *next_ref,
):
    modes = dec_ref.shape[0]
    there = there_ref.at[0:modes, :]
    after_ref[...] = later_step(me_ref, there, later_ref[...], dec_ref, length, tokens, hop)
    state = suffix_step(me_ref, there[...].astype(F32), state_ref[...], dec_ref, length, tokens, hop)
    if next_ref:
        next_ref[0][...] = state
    sent_ref[0:modes, :] = state.astype(BF16)
    sums = sums_ref[...] + there_ref[modes:, :].astype(F32)
    total_ref[...] = sums
    sent_ref[modes:, :] = sums.astype(BF16)


def tail_step(me, there, state, later, sums, decays, tokens, length, hop, more):
    args = (there, state, later, sums, decays)
    outs = (there, later, sums) + ((state,) if more else ())
    return pl.pallas_call(
        functools.partial(tail_kernel, length, tokens, hop),
        out_shape=tuple(jax.ShapeDtypeStruct(x.shape, x.dtype) for x in outs),
        in_specs=[SM] + [VM] * 5,
        out_specs=(VM,) * len(outs),
        compiler_params=params(),
        cost_estimate=SMALL,
        name="tail_step",
    )(me, *args)


def sum_kernel(there_ref, sums_ref, sent_ref, total_ref):
    sums = sums_ref[...] + there_ref[there_ref.shape[0] - sums_ref.shape[0] :, :].astype(F32)
    total_ref[...] = sums
    sent_ref[...] = sums.astype(BF16)


def sum_step(there, sums):
    return pl.pallas_call(
        sum_kernel,
        out_shape=(jax.ShapeDtypeStruct(sums.shape, BF16), jax.ShapeDtypeStruct(sums.shape, F32)),
        in_specs=[VM] * 2,
        out_specs=(VM,) * 2,
        compiler_params=params(),
        cost_estimate=SMALL,
        name="sum_step",
    )(there, sums)


def result_kernel(length, there_ref, sums_ref, res_ref, ores_ref, odec_ref, oskip_ref):
    modes = res_ref.shape[0]
    sums = sums_ref[...] + there_ref[...].astype(F32)
    ores_ref[...] = sums[0:modes] * (1.0 / length)
    odec_ref[...] = sums[modes : 2 * modes] * (-1.0 / (length * length)) * res_ref[...]
    oskip_ref[...] = sums[2 * modes : 2 * modes + 1] * (1.0 / math.sqrt(length))


def results(there, sums, residues, length):
    modes, width = residues.shape
    return pl.pallas_call(
        functools.partial(result_kernel, length),
        out_shape=(
            jax.ShapeDtypeStruct((modes, width), F32),
            jax.ShapeDtypeStruct((modes, width), F32),
            jax.ShapeDtypeStruct((1, width), F32),
        ),
        in_specs=[VM] * 3,
        out_specs=(VM,) * 3,
        compiler_params=params(),
        cost_estimate=SMALL,
        name="results",
    )(there, sums, residues)


def prefix_step(me, there, state, carried, decays, tokens, length, hop, more):
    args = [there, state, *carried, decays]
    dtypes = (BF16, F32, F32) if more else (BF16, F32)
    return pl.pallas_call(
        functools.partial(prefix_kernel, length, tokens, hop, len(carried)),
        out_shape=tuple(jax.ShapeDtypeStruct(state.shape, dtype) for dtype in dtypes),
        in_specs=[SM] + [VM] * len(args),
        out_specs=(VM,) * len(dtypes),
        compiler_params=params(),
        cost_estimate=SMALL,
        name="prefix_step",
    )(me, *args)


def join_kernel(chunks, *refs):
    sent_ref, state_ref = refs[len(chunks) :]
    for part_ref, (low, high) in zip(refs, chunks):
        state_ref[:, low:high] = part_ref[...]
        sent_ref[:, low:high] = part_ref[...].astype(BF16)


def join_states(states, chunks):
    modes, width = states[0].shape[0], chunks[-1][1]
    return pl.pallas_call(
        functools.partial(join_kernel, chunks),
        out_shape=tuple(jax.ShapeDtypeStruct((modes, width), dtype) for dtype in (BF16, F32)),
        in_specs=[VM] * len(states),
        out_specs=(VM,) * 2,
        compiler_params=params(),
        cost_estimate=SMALL,
        name="join_states",
    )(*states)


def weight_copies(blocks_ref, w_ref, width, targets, sems):
    copies = []
    for q, target in enumerate(targets):
        start = pl.multiple_of(blocks_ref[q] * width, width)
        copies.append(pltpu.make_async_copy(w_ref.at[pl.ds(start, width)], target, sems.at[q]))
    return copies


def project_block(up_ref, w_rows, out_ref):
    width = w_rows.shape[0]
    rows = min(width, 256)
    for start in range(0, width, rows):
        out_ref[:, start : start + rows] = lax.dot_general(
            up_ref[...], w_rows[start : start + rows, :], (((1,), (1,)), ((), ())),
            preferred_element_type=F32,
        ).astype(out_ref.dtype)


def fetch_kernel(blocks_ref, w_ref, o_ref, sems):
    pieces = blocks_ref.shape[0]
    width = o_ref.shape[0] // pieces
    targets = [o_ref.at[q * width : (q + 1) * width, :] for q in range(pieces)]
    copies = weight_copies(blocks_ref, w_ref, width, targets, sems)
    for copy in copies:
        copy.start()
    for copy in copies:
        copy.wait()


def fetch(weight, width, blocks):
    pieces = blocks.shape[0]
    return pl.pallas_call(
        fetch_kernel,
        out_shape=jax.ShapeDtypeStruct((pieces * width, weight.shape[1]), BF16),
        in_specs=[SM, HBM],
        out_specs=VM,
        scratch_shapes=[pltpu.SemaphoreType.DMA((pieces,))],
        compiler_params=params(PROJECT_LIMIT),
        cost_estimate=takes(3),
        name="fetch",
    )(blocks, weight)


def multiply_kernel(up_ref, held_ref, o_ref):
    project_block(up_ref, held_ref, o_ref)


def multiply(up, held):
    return pl.pallas_call(
        multiply_kernel,
        out_shape=jax.ShapeDtypeStruct((up.shape[0], held.shape[0]), BF16),
        in_specs=[VM] * 2,
        out_specs=VM,
        compiler_params=params(),
        cost_estimate=takes(1),
        name="multiply",
    )(up, held)


def scan_kernel(pieces, chunks, length, blocks_ref, up_ref, w_ref, sig_ref, dec_ref, *refs):
    outs, (end_ref, sent_ref, *tables) = refs[:pieces], refs[pieces:-4]
    w_buf, sems, ebuf, e1buf = refs[-4:]
    width = w_buf.shape[1]
    copies = weight_copies(blocks_ref, w_ref, width, [w_buf.at[q] for q in range(pieces)], sems)
    for copy in copies:
        copy.start()
    for k, (low, high) in enumerate(chunks):
        signal_chunk(length, low, high, sig_ref, dec_ref, end_ref, *tables[3 * k : 3 * k + 3], ebuf, e1buf)
    sent_ref[...] = end_ref[...].astype(BF16)
    for copy in copies:
        copy.wait()
    for q, out in enumerate(outs):
        project_block(up_ref, w_buf.at[q], out)


def project_and_scan(up, weight, width, blocks, signal, decays, chunks, length):
    tokens, feats = up.shape
    modes = decays.shape[0]
    pieces = blocks.shape[0]
    shapes = [jax.ShapeDtypeStruct((tokens, width), BF16)] * pieces
    shapes += [jax.ShapeDtypeStruct((2 * modes, width), dtype) for dtype in (F32, BF16)]
    for low, high in chunks:
        states = jax.ShapeDtypeStruct((modes * SUB, high - low), BF16)
        shapes += [jax.ShapeDtypeStruct((tokens, high - low), BF16), states, states]
    out = pl.pallas_call(
        functools.partial(scan_kernel, pieces, chunks, length),
        out_shape=shapes,
        in_specs=[SM, VM, HBM, VM, VM],
        out_specs=[VM] * len(shapes),
        scratch_shapes=[
            pltpu.VMEM((pieces, width, feats), BF16),
            pltpu.SemaphoreType.DMA((pieces,)),
        ]
        + [pltpu.VMEM((modes * SUB, LANES), F32)] * 2,
        compiler_params=params(PROJECT_LIMIT),
        cost_estimate=takes(6),
        name="project_and_scan",
    )(blocks, up, weight, signal, decays)
    tables = out[pieces + 2 :]
    return out[:pieces], out[pieces : pieces + 2], [
        tables[3 * k : 3 * k + 3] for k in range(len(chunks))
    ]


def last_kernel(block_ref, up_ref, w_ref, o_ref, w_buf, sems):
    (copy,) = weight_copies(block_ref, w_ref, w_buf.shape[0], [w_buf], sems)
    copy.start()
    copy.wait()
    project_block(up_ref, w_buf, o_ref)


def project_last(up, weight, width, block):
    tokens, feats = up.shape
    return pl.pallas_call(
        last_kernel,
        out_shape=jax.ShapeDtypeStruct((tokens, width), BF16),
        in_specs=[SM, VM, HBM],
        out_specs=VM,
        scratch_shapes=[pltpu.VMEM((width, feats), BF16), pltpu.SemaphoreType.DMA((1,))],
        compiler_params=params(PROJECT_LIMIT),
        cost_estimate=takes(4),
        name="project_last",
    )(block, up, weight)


def pair_kernel(chunks, lent, mine_ref, lent_ref, *outs):
    base = mine_ref.shape[1] * lent
    for (low, high), out in zip(chunks, outs):
        total = mine_ref[:, low:high].astype(F32) + lent_ref[:, base + low : base + high].astype(F32)
        out[...] = total.astype(BF16)


def pair_sums(mine, lent, index, chunks):
    tokens = mine.shape[0]
    return pl.pallas_call(
        functools.partial(pair_kernel, chunks, index),
        out_shape=[jax.ShapeDtypeStruct((tokens, high - low), BF16) for low, high in chunks],
        in_specs=[VM] * 2,
        out_specs=[VM] * len(chunks),
        compiler_params=params(),
        cost_estimate=SMALL,
        name="pair_sums",
    )(mine, lent)


def send(x, axis, size, hop):
    return lax.ppermute(x, axis, [(i, i ^ hop) for i in range(size)])


def cuts(width):
    lane_blocks = width // LANES
    first = lane_blocks // 2 * LANES
    return [(0, first), (first, width)]


def body(signal, upstream, out_weight, residues, decays, skip_gain):
    tokens, width = signal.shape
    groups = lax.axis_size("ctx")
    blocks = lax.axis_size("ch")
    length = tokens * groups
    modes = residues.shape[1]
    me = lax.axis_index("ch")
    place = jnp.reshape(lax.axis_index("ctx").astype(jnp.int32), (1,))
    dec = decays.T
    res = residues.T
    gain = skip_gain[None, :]
    chunks = cuts(width)
    hops = range(2, blocks, 2)
    levels = [1 << k for k in range(groups.bit_length() - 1)]

    index = lambda blocks: jnp.stack(blocks).astype(jnp.int32)
    first, second, third = index([me ^ hop ^ 1 for hop in hops]), index([me ^ hop for hop in hops] + [me ^ 1]), index([me])
    first, second, third, place = lax.optimization_barrier((first, second, third, place))
    lent = send(multiply(upstream, fetch(out_weight, width, first)), "ch", blocks, 1)
    (*parts, mine), (state, sent), tables = project_and_scan(
        upstream, out_weight, width, second, signal, dec, chunks, length
    )
    pairs = [pair_sums(part, lent, index, chunks) for index, part in enumerate(parts)]
    upstream, pairs = lax.optimization_barrier((upstream, pairs))
    arrived = [[send(pair[k], "ch", blocks, hop) for pair, hop in zip(pairs, hops)] for k in range(len(chunks))]
    own = project_last(upstream, out_weight, width, third)
    lent = send(mine, "ch", blocks, 1)

    before, pays, states, locs = [], [], [], []

    def take(chunk, low, high, sigp, y, y1):
        grad, z, own_state = gradient_states([own, lent, *chunk], high - low, low, dec, length)
        states.append(own_state)
        pays.append(filter_sums(grad, sigp, dec, y, y1, length, low))
        locs.append((grad, z, low))

    for hop in levels:
        if hop == levels[-1]:
            sent, own = lax.optimization_barrier((sent, own))
            pass
        there = send(sent, "ctx", groups, hop)
        if hop == 1:
            there, pairs = lax.optimization_barrier((there, pairs))
        if hop != levels[-1]:
            sent, after, *rest = prefix_step(
                place, there, state, before, dec, tokens, length, hop, hop * 2 != levels[-1]
            )
            state, before = (rest + [None])[0], [after]
    ends = there
    for k in range(len(pays), len(chunks)):
        pays, arrived[k] = lax.optimization_barrier((pays, arrived[k]))
        take(arrived[k], *chunks[k], *tables[k])
    sent, state = join_states(states, chunks)
    locs, reaches = zip(*[local_part(grad, z, dec, res, gain, length, low) for grad, z, low in locs])
    there = send(sent, "ctx", groups, levels[0])
    sent, state, later, sums = merge(
        place, there, state, ends, pays, dec, before, chunks, tokens, length, levels[0], levels[-1]
    )
    for hop in levels[1:]:
        there = send(sent, "ctx", groups, hop)
        if hop != levels[-1]:
            sent, later, sums, *state = tail_step(
                place, there, state, later, sums, dec, tokens, length, hop, hop * 2 != levels[-1]
            )
            state = state[0] if state else None
    moved, sums = sum_step(there, sums)
    out = finish(place, there, later, dec, locs, reaches, chunks, tokens, length, levels[-1])
    ores, odec, oskip = results(send(moved, "ctx", groups, levels[0]), sums, res, length)
    return (out, ores.T, odec.T, oskip[0])


def solution(mesh):
    placed = (P("ctx", "ch"), P("ctx", "ch"), P(None, "ch"), P("ch", None), P("ch", None), P("ch"))
    return jax.shard_map(
        body,
        mesh=mesh,
        in_specs=placed,
        out_specs=(P("ctx", "ch"), P("ch", None), P("ch", None), P("ch")),
        check_vma=False,
    )
```
